256 devices in a mesh: gx: 32 (over z_lo, y, core), gy: 8 (over x, z_hi).
Axes of the slice: x: 4, y: 4, z: 8 (z_hi: 2, z_lo: 4; z = z_hi * 4 + z_lo), core: 2. Of those that a mesh axis runs over, the one named last changes fastest.
Arguments:
- node_cells: int32 [3, 1048576], P(None, ('gx', 'gy')), may hold values from 0 to 191, as said below
- node_frac: float32 [3, 1048576], P(None, ('gx', 'gy')), may hold values from 0 to 1
- node_force: float32 [1048576], P(('gx', 'gy')), may hold values from -6 to 6
- node_count: int32 [256], P(('gx', 'gy')), may hold values from 1 to 4096, as said below
- z_rates: float32 [64], replicated, may hold values from 0.1 to 4
- z_synth: float32 [64, 64], replicated, may hold values from -0.75 to 0.75
- z_analysis: float32 [64, 64], replicated, may hold values from -0.75 to 0.75
Outputs:
- velocity_modes: float32 [2, 64, 1536, 1536], P(None, None, ('gx', 'gy'))
The draws below stay inside these ranges and needn't reach their ends.
Inputs may be any that keep to these rules, and one draw needn't show every extreme that they name: `node_cells`: rows are x, y, z; x below 48, y below 192, z at most 58. `node_count`: some device holds 4096 live nodes in every draw.
All inputs are finite; a program needn't handle non-finite values.
Results may differ from the reference program's by a relative error of at most 0.003.
Values may be sent and summed in bfloat16 or wider, within the bound.
No kernel may reach another device: no remote copies, remote signals or barrier semaphores. Data moves between devices by JAX's collectives and lax.ppermute only.
A program may use at most 128 MiB of HBM per device.

```python
import math
import jax
import jax.numpy as jnp
from jax import lax

NX = 1536
NY = 1536
NZ = 64
WIN = 6
NODE_CAP = 4096
CX = 48
CY = 192
NODES = 1048576
N_GX = 32
N_GY = 8


def draw_node_count(key, part):
    devices = N_GX * N_GY
    key_base = jax.random.fold_in(key, 11)
    key_shift = jax.random.fold_in(key, 12)
    key_full = jax.random.fold_in(key, 13)
    base_count = jax.random.randint(key_base, (devices,), 1, NODE_CAP + 1)
    halvings = jax.random.randint(key_shift, (devices,), 0, 3)
    counts = jnp.maximum(base_count // jnp.power(2, halvings), 1)
    full_device = jax.random.randint(key_full, (), 0, devices)
    return jnp.where(jnp.arange(devices) == full_device, NODE_CAP, counts).astype(jnp.int32)


def draw_node_cells(key, part):
    key_x = jax.random.fold_in(key, 21)
    key_y = jax.random.fold_in(key, 22)
    key_z = jax.random.fold_in(key, 23)
    row_x = jax.random.randint(key_x, (NODES,), 0, CX)
    row_y = jax.random.randint(key_y, (NODES,), 0, CY)
    row_z = jax.random.randint(key_z, (NODES,), 0, NZ - WIN + 1)
    return jnp.stack([row_x, row_y, row_z]).astype(jnp.int32)


def shard_levels(stream_key, extent, shards, smallest, top_value):
    level, own = 1.0, jax.random.fold_in(stream_key, 6)
    for axis_at, parts in shards:
        draws = jnp.exp(jax.random.uniform(jax.random.fold_in(own, axis_at), (parts,), jnp.float32, smallest / len(shards), top_value / len(shards)))
        level = level * jnp.repeat(draws, extent[axis_at] // parts).reshape([-1 if axis == axis_at else 1 for axis in range(len(extent))])
    return level


def normal_values(stream_key, shape, scale, limit, split=(), kind=jnp.bfloat16):
    result = jax.random.normal(stream_key, shape, jnp.float32) * scale
    if len(split) > 0:
        result = shard_levels(stream_key, shape, split, -0.22, 0.18) * result
    return jnp.clip(result, min=-limit, max=limit).astype(kind)


def setup_inputs(seed: int = 0) -> dict:
    splits = jax.random.split(jax.random.key(seed), 8)
    return {
        "node_cells": draw_node_cells(jax.random.fold_in(splits[7], 71), 0),
        "node_frac": jnp.clip(1.0 * jax.random.uniform(splits[1], (3, NODES), jnp.float32) ** shard_levels(splits[1], (3, NODES), ((1, 256),), -0.2, 0.2), 0.0, 1.0),
        "node_force": normal_values(splits[2], (NODES,), 1.0, 6.0, ((0, 256),), jnp.float32),
        "node_count": draw_node_count(jax.random.fold_in(splits[7], 71), 0),
        "z_rates": jnp.clip(jnp.exp(jax.random.uniform(splits[4], (NZ,), jnp.float32, math.log(0.1), math.log(4.0))), 0.1, 4.0),
        "z_synth": normal_values(splits[5], (NZ, NZ), NZ ** -0.5, 0.75, (), jnp.float32),
        "z_analysis": normal_values(splits[6], (NZ, NZ), NZ ** -0.5, 0.75, (), jnp.float32),
    }


def window_weights(frac_row, width):
    offsets = jnp.arange(width, dtype=jnp.float32)
    distance = offsets[None, :] - (width - 1) / 2.0 - frac_row[:, None]
    return jnp.exp(-distance * distance / 2.0)

def reference(node_cells, node_frac, node_force, node_count, z_rates, z_synth, z_analysis):
    devices = N_GX * N_GY
    capacity = NODE_CAP
    scale = 8.0 / math.sqrt(NODE_CAP * devices)
    offsets = jnp.arange(WIN, dtype=jnp.int32)

    def one_device(grid_flat, device):
        first_slot = (device * capacity).astype(jnp.int32)
        cell_rows = lax.dynamic_slice_in_dim(node_cells, first_slot, capacity, 1)
        frac_rows = lax.dynamic_slice_in_dim(node_frac, first_slot, capacity, 1)
        forces = lax.dynamic_slice_in_dim(node_force, first_slot, capacity, 0)
        live = jnp.arange(capacity, dtype=jnp.int32) < node_count[device]
        weighted = jnp.where(live, forces * scale, 0.0)
        x_weights = window_weights(frac_rows[0], WIN)
        y_weights = window_weights(frac_rows[1], WIN)
        z_weights = window_weights(frac_rows[2], WIN)
        outer_left = ((weighted[:, None] * z_weights)[:, :, None] * x_weights[:, None, :]).astype(jnp.bfloat16)
        outer_right = y_weights.astype(jnp.bfloat16)
        values = outer_left.astype(jnp.float32)[:, :, :, None] * outer_right.astype(jnp.float32)[:, None, None, :]
        slab_index = device // N_GY
        strip_index = device % N_GY
        z_index = cell_rows[2][:, None] + offsets[None, :]
        x_index = (slab_index * CX + cell_rows[0][:, None] + offsets[None, :]) % NX
        y_index = (strip_index * CY + cell_rows[1][:, None] + offsets[None, :]) % NY
        flat_index = (z_index[:, :, None, None] * NX + x_index[:, None, :, None]) * NY + y_index[:, None, None, :]
        grid_flat = grid_flat.at[flat_index.reshape(-1).astype(jnp.int32)].add(values.reshape(-1))
        return (grid_flat, None)
    grid_flat, _ = lax.scan(one_device, jnp.zeros((NZ * NX * NY,), jnp.float32), jnp.arange(devices, dtype=jnp.int32))
    grid_low = grid_flat.reshape(NZ, NX, NY).astype(jnp.bfloat16)
    grid_low = lax.optimization_barrier(grid_low)
    y_modes = jnp.fft.fft(grid_low.astype(jnp.float32), axis=2)
    y_real = jnp.real(y_modes).astype(jnp.bfloat16)
    y_imag = jnp.imag(y_modes).astype(jnp.bfloat16)
    y_real, y_imag = lax.optimization_barrier((y_real, y_imag))
    xy_modes = jnp.fft.fft(lax.complex(y_real.astype(jnp.float32), y_imag.astype(jnp.float32)), axis=1)
    modes_real = jnp.real(xy_modes)
    modes_imag = jnp.imag(xy_modes)
    x_wave = jnp.sin(jnp.pi * jnp.arange(NX, dtype=jnp.float32) / NX)
    y_wave = jnp.sin(jnp.pi * jnp.arange(NY, dtype=jnp.float32) / NY)
    wave_sq = 4.0 * (x_wave[:, None] * x_wave[:, None] + y_wave[None, :] * y_wave[None, :])
    denominator = wave_sq[None, :, :] + z_rates[:, None, None]
    highest = lax.Precision.HIGHEST
    coef_real = jnp.einsum('az,zxy->axy', z_analysis, modes_real, precision=highest) / denominator
    coef_imag = jnp.einsum('az,zxy->axy', z_analysis, modes_imag, precision=highest) / denominator
    velocity_real = jnp.einsum('za,axy->zxy', z_synth, coef_real, precision=highest)
    velocity_imag = jnp.einsum('za,axy->zxy', z_synth, coef_imag, precision=highest)
    return jnp.transpose(jnp.stack([velocity_real, velocity_imag]), (0, 1, 3, 2))
```

```python
import functools
import math

import jax
import jax.numpy as jnp
import numpy as np
from jax import lax
from jax.experimental import pallas as pl
from jax.experimental.pallas import tpu as pltpu
from jax.sharding import PartitionSpec as P

NX = 1536
NY = 1536
WIN = 6
NZ = 64
RADIX = 6
BASE = 256
SLAB = 48
STRIP = 192
ROWS = 208
LANES = 128
NODE_BLOCK = 1024
GROUPS = ((0, 1, 2),)
BOTH = ("gx", "gy")
F32 = jnp.float32
BF16 = jnp.bfloat16
HALF_ROOT3 = math.sqrt(3.0) / 2.0
VMEM_BYTES = 56 * 1024 * 1024


def split_table(table):
    high = table.astype(np.float32).astype(BF16)
    low = (table - high.astype(np.float64)).astype(np.float32).astype(BF16)
    return high, low


def base_tables():
    index = np.arange(BASE)
    angle = 2.0 * np.pi * (np.outer(index, index) % BASE) / BASE
    return np.cos(angle), np.sin(angle)


def split_value(value):
    high = value.astype(BF16)
    return high, (value - high.astype(F32)).astype(BF16)


def window(position, cell, frac):
    offset = position - cell
    distance = offset.astype(F32) - (WIN - 1) / 2.0 - frac
    inside = (offset >= 0) & (offset < WIN)
    return jnp.where(inside, jnp.exp(-distance * distance / 2.0), 0.0)


def dot_rows(left, right):
    return lax.dot_general(left, right, (((1,), (1,)), ((), ())), preferred_element_type=F32)


def matmul(left, right):
    return jnp.dot(left, right, preferred_element_type=F32)


def block_count(count_ref):
    return (count_ref[0] + (NODE_BLOCK - 1)) >> (NODE_BLOCK.bit_length() - 1)


def prepare_kernel(
    count_ref, cell_ref, frac_ref, force_ref, right_ref, z_ref, x_ref, rim_ref, left_ref, sum_ref
):
    live_count = count_ref[0]
    capacity = force_ref.shape[1]
    scale = 8.0 / math.sqrt(capacity * 256)
    sum_ref[...] = jnp.zeros_like(sum_ref)

    def body(block, carry):
        start = pl.multiple_of(block * NODE_BLOCK, NODE_BLOCK)
        span = pl.ds(start, NODE_BLOCK)

        def rows(extent):
            return lax.broadcasted_iota(jnp.int32, (extent, NODE_BLOCK), 0)

        slot = start + lax.broadcasted_iota(jnp.int32, (1, NODE_BLOCK), 1)
        amplitude = jnp.where(slot < live_count, force_ref[:, span] * scale, 0.0)
        z_part = amplitude * window(rows(NZ), cell_ref[2:3, span], frac_ref[2:3, span])
        x_part = window(rows(56), cell_ref[0:1, span], frac_ref[0:1, span])
        right = window(rows(ROWS), cell_ref[1:2, span], frac_ref[1:2, span]).astype(BF16)
        z_ref[:, span] = z_part
        x_ref[:, span] = x_part
        right_ref[:, span] = right
        for t in range(RADIX):
            left_ref[t * NZ : (t + 1) * NZ, :] = (
                z_part * x_part[SLAB + t : SLAB + t + 1, :]
            ).astype(BF16)
        sum_ref[...] += dot_rows(right, left_ref[...])
        return carry

    lax.fori_loop(0, block_count(count_ref), body, 0)
    rim_ref[...] = sum_ref[...].astype(BF16)


def spread_kernel(pairs, count_ref, right_ref, z_ref, x_ref, out_ref, left_ref, sum_ref):
    width = len(pairs) * LANES
    sum_ref[...] = jnp.zeros_like(sum_ref)

    def body(block, carry):
        span = pl.ds(pl.multiple_of(block * NODE_BLOCK, NODE_BLOCK), NODE_BLOCK)

        def step(half, inner):
            for k in range(2):
                for p, pair in enumerate(pairs):
                    for par in range(2):
                        x_at = (2 * half + k) * RADIX + 2 * pair + par
                        row = ((k * len(pairs) + p) * 2 + par) * NZ
                        left_ref[row : row + NZ, :] = (
                            z_ref[:, span] * x_ref[pl.ds(x_at, 1), span]
                        ).astype(BF16)
            lanes = pl.ds(pl.multiple_of(half * 2 * width, LANES), 2 * width)
            sum_ref[:, lanes] += dot_rows(right_ref[:, span], left_ref[...])
            return inner

        return lax.fori_loop(0, 4, step, carry)

    lax.fori_loop(0, block_count(count_ref), body, 0)
    for j in range(8):
        out_ref[j] = sum_ref[:, j * width : (j + 1) * width].astype(BF16)


def y_kernel(
    in_ref, high_ref, low_ref, cos_ref, sin_ref, out_ref, grid_ref, th_ref, tl_ref
):
    width = in_ref.shape[2]
    pair_count = width // LANES
    for j in range(8):
        grid_ref[j * STRIP : (j + 1) * STRIP, :] = in_ref[j, 0:STRIP, :].astype(F32)
    for j in range(8):
        before = (j + 7) % 8
        grid_ref[j * STRIP : j * STRIP + 16, :] += in_ref[before, STRIP:ROWS, :].astype(F32)

    def body(step, carry):
        start = pl.multiple_of(step * 16, 16)
        for p in range(pair_count):
            lanes = slice(p * LANES, (p + 1) * LANES)
            a = [grid_ref[pl.ds(n * BASE + start, 16), lanes] for n in range(RADIX)]
            s0, s1, s2 = a[0] + a[3], a[1] + a[4], a[2] + a[5]
            d0, d1, d2 = a[0] - a[3], a[1] - a[4], a[2] - a[5]
            h1r, h1i = d0 + 0.5 * (d1 - d2), -HALF_ROOT3 * (d1 + d2)
            h2r, h2i = s0 - 0.5 * (s1 + s2), -HALF_ROOT3 * (s1 - s2)
            turned = (
                (s0 + s1 + s2, None),
                (h1r, h1i),
                (h2r, h2i),
                (d0 - d1 + d2, None),
                (h2r, -h2i),
                (h1r, -h1i),
            )
            for q, (real, imag) in enumerate(turned):
                if q > 0:
                    cos = cos_ref[q - 1, pl.ds(start, 16), :]
                    sin = sin_ref[q - 1, pl.ds(start, 16), :]
                    if imag is None:
                        real, imag = real * cos, -real * sin
                    else:
                        real, imag = real * cos + imag * sin, imag * cos - real * sin
                else:
                    imag = jnp.zeros_like(real)
                columns = slice(q * width + p * LANES, q * width + (p + 1) * LANES)
                for at, value in ((0, real), (BASE, imag)):
                    high, low = split_value(value)
                    th_ref[pl.ds(at + start, 16), columns] = high
                    tl_ref[pl.ds(at + start, 16), columns] = low
        return carry

    lax.fori_loop(0, BASE // 16, body, 0)
    for pair in range(3):
        columns = slice(2 * pair * width, 2 * (pair + 1) * width)
        high = th_ref[:, columns]
        modes = matmul(high_ref[...], high)
        modes += matmul(low_ref[...], high)
        modes += matmul(high_ref[...], tl_ref[:, columns])
        for k in range(2):
            q = 2 * pair + k
            for part in range(2):
                for p in range(pair_count):
                    at = (k * pair_count + p) * LANES
                    out_ref[(q * 2 + part) * pair_count + p] = modes[
                        part * BASE : (part + 1) * BASE, at : at + LANES
                    ].astype(BF16)


def x_kernel(
    group_count,
    *refs,
):
    in_refs = refs[:group_count]
    (
        wave_ref,
        high_ref,
        low_ref,
        cos_ref,
        sin_ref,
        across_ref,
        rate_ref,
        analysis_ref,
        synth_ref,
        out_ref,
        modes_ref,
        x_ref,
        c_ref,
        wa_ref,
        ws_ref,
    ) = refs[group_count:]
    per_group = 3 // group_count
    q = pl.program_id(0)

    @pl.when(q == 0)
    def _():
        high, low = split_value(analysis_ref[...])
        for k in range(2):
            wa_ref[k * LANES : (k + 1) * LANES, :LANES] = high
            wa_ref[k * LANES : (k + 1) * LANES, LANES:] = low
        high, low = split_value(synth_ref[...])
        for k in range(2):
            ws_ref[:LANES, k * LANES : (k + 1) * LANES] = high
            ws_ref[LANES:, k * LANES : (k + 1) * LANES] = low

    lines = jnp.concatenate(
        [
            in_refs[xp // per_group][part * per_group + xp % per_group]
            for part in range(2)
            for xp in range(3)
        ],
        axis=1,
    )
    modes_ref[...] = matmul(high_ref[...], lines) + matmul(low_ref[...], lines)
    lane = lax.broadcasted_iota(jnp.int32, (16, LANES), 1)
    lower = lane < NZ
    sign = jnp.where(lower, 1.0, -1.0)
    turn_1r = jnp.where(lower, 1.0, 0.5)
    turn_2r = jnp.where(lower, 1.0, -0.5)
    turn_i = jnp.where(lower, 0.0, -HALF_ROOT3)

    def body(step, carry):
        start = pl.multiple_of(step * 16, 16)
        real, imag = [], []
        for xp in range(3):
            at_real = slice(xp * LANES, (xp + 1) * LANES)
            at_imag = slice((3 + xp) * LANES, (4 + xp) * LANES)
            mode_real = (
                modes_ref[pl.ds(start, 16), at_real] + modes_ref[pl.ds(BASE + start, 16), at_imag]
            )
            mode_imag = (
                modes_ref[pl.ds(start, 16), at_imag] - modes_ref[pl.ds(BASE + start, 16), at_real]
            )
            cos = cos_ref[xp, pl.ds(start, 16), :]
            sin = sin_ref[xp, pl.ds(start, 16), :]
            real.append(mode_real * cos + mode_imag * sin)
            imag.append(mode_imag * cos - mode_real * sin)
        sum_r, sum_i = real[1] + real[2], imag[1] + imag[2]
        dif_r, dif_i = HALF_ROOT3 * (real[1] - real[2]), HALF_ROOT3 * (imag[1] - imag[2])
        mid_r, mid_i = real[0] - 0.5 * sum_r, imag[0] - 0.5 * sum_i
        u1r, u1i = mid_r + dif_i, mid_i - dif_r
        u2r, u2i = mid_r - dif_i, mid_i + dif_r
        thirds = (
            (real[0] + sum_r, imag[0] + sum_i),
            (u1r * turn_1r - u1i * turn_i, u1i * turn_1r + u1r * turn_i),
            (u2r * turn_2r - u2i * turn_i, u2i * turn_2r + u2r * turn_i),
        )
        for m in range(3):
            for part in range(2):
                value = thirds[m][part]
                value = pltpu.roll(value, NZ, 1) + sign * value
                high, low = split_value(value)
                row = pl.ds((m * 2 + part) * BASE + start, 16)
                x_ref[row, :LANES] = high
                x_ref[row, LANES:] = low
        return carry

    lax.fori_loop(0, BASE // 16, body, 0)
    shift = rate_ref[...] + wave_ref[q]
    for m in range(3):
        inverse = 1.0 / (across_ref[m] + shift)
        for part in range(2):
            rows = slice((m * 2 + part) * BASE, (m * 2 + part + 1) * BASE)
            both = matmul(x_ref[rows, :], wa_ref[...])
            high, low = split_value((both[:, :LANES] + both[:, LANES:]) * inverse)
            c_ref[rows, :LANES] = high
            c_ref[rows, LANES:] = low
            both = dot_rows(ws_ref[...], c_ref[rows, :])
            value = both[:LANES] + both[LANES:]
            out_ref[part, 0, :, m * BASE : (m + 1) * BASE] = value[:NZ]
            out_ref[part, 0, :, (m + 3) * BASE : (m + 4) * BASE] = value[NZ:]


def vmem_call(kernel, inputs, out_shape, scratch_shapes, scalars=1, cost=None):
    specs = [pl.BlockSpec(memory_space=pltpu.SMEM)] * scalars
    specs += [pl.BlockSpec(memory_space=pltpu.VMEM)] * (len(inputs) - scalars)
    return pl.pallas_call(
        kernel,
        out_shape=out_shape,
        in_specs=specs,
        out_specs=jax.tree.map(lambda _: pl.BlockSpec(memory_space=pltpu.VMEM), out_shape),
        scratch_shapes=scratch_shapes,
        compiler_params=pltpu.CompilerParams(vmem_limit_bytes=VMEM_BYTES),
        cost_estimate=cost,
    )(*inputs)


def twin(matrix):
    zero = jnp.zeros_like(matrix)
    return jnp.concatenate(
        [jnp.concatenate([matrix, zero], axis=1), jnp.concatenate([zero, matrix], axis=1)], axis=0
    )


def shards(node_cells, node_frac, node_force, node_count, z_rates, z_synth, z_analysis):
    capacity = node_force.shape[0]
    slabs = lax.axis_size("gx")
    cos_base, sin_base = base_tables()
    full = np.block([[cos_base, sin_base], [-sin_base, cos_base]])
    full_high, full_low = split_table(full)
    half_high, half_low = split_table(np.concatenate([cos_base, sin_base], axis=0))

    right, z_part, x_part, rim = vmem_call(
        prepare_kernel,
        (node_count, node_cells, node_frac, node_force.reshape(1, capacity)),
        (
            jax.ShapeDtypeStruct((ROWS, capacity), BF16),
            jax.ShapeDtypeStruct((NZ, capacity), F32),
            jax.ShapeDtypeStruct((56, capacity), F32),
            jax.ShapeDtypeStruct((ROWS, RADIX * NZ), BF16),
        ),
        [
            pltpu.VMEM((RADIX * NZ, NODE_BLOCK), BF16),
            pltpu.VMEM((ROWS, RADIX * NZ), F32),
        ],
        cost=pl.CostEstimate(flops=10**9, bytes_accessed=10**7, transcendentals=10**6),
    )
    rim = lax.ppermute(rim, "gx", [(i, (i + 1) % slabs) for i in range(slabs)])

    row = np.arange(BASE)
    angle = 2.0 * np.pi * np.outer(np.arange(1, RADIX), row) / NY
    y_cos = np.broadcast_to(np.cos(angle)[:, :, None], (RADIX - 1, BASE, LANES)).astype(np.float32)
    y_sin = np.broadcast_to(np.sin(angle)[:, :, None], (RADIX - 1, BASE, LANES)).astype(np.float32)

    arrived = []
    for pairs in GROUPS:
        width = len(pairs) * LANES
        tiles = vmem_call(
            functools.partial(spread_kernel, pairs),
            (node_count, right, z_part, x_part),
            jax.ShapeDtypeStruct((8, ROWS, width), BF16),
            [
                pltpu.VMEM((2 * width, NODE_BLOCK), BF16),
                pltpu.VMEM((ROWS, 8 * width), F32),
            ],
            cost=pl.CostEstimate(
                flops=10**10 // len(GROUPS), bytes_accessed=10**7, transcendentals=0
            ),
        )
        rim_lanes = rim[:, pairs[0] * LANES : (pairs[-1] + 1) * LANES]
        tiles = tiles.at[0].set((tiles[0].astype(F32) + rim_lanes.astype(F32)).astype(BF16))
        lines = lax.all_to_all(tiles, "gy", split_axis=0, concat_axis=0, tiled=True)
        items = 2 * RADIX * len(pairs)
        spectrum = vmem_call(
            y_kernel,
            (lines, full_high, full_low, y_cos, y_sin),
            jax.ShapeDtypeStruct((items, BASE, LANES), BF16),
            [
                pltpu.VMEM((NY, width), F32),
                pltpu.VMEM((2 * BASE, RADIX * width), BF16),
                pltpu.VMEM((2 * BASE, RADIX * width), BF16),
            ],
            scalars=0,
            cost=pl.CostEstimate(
                flops=5 * 10**9 // len(GROUPS), bytes_accessed=10**7, transcendentals=0
            ),
        )
        packed = spectrum.reshape(items // 4, 4, BASE, LANES).transpose(2, 0, 1, 3)
        moved = lax.all_to_all(packed, BOTH, split_axis=0, concat_axis=0, tiled=True)
        arrived.append(moved.transpose(1, 2, 0, 3).reshape(items, BASE, LANES))

    offset = np.arange(RADIX).reshape(3, 2)
    angle = 2.0 * np.pi * offset[:, None, :] * row[None, :, None] / NX
    x_cos = np.repeat(np.cos(angle), NZ, axis=2).astype(np.float32)
    x_sin = np.repeat(np.sin(angle), NZ, axis=2).astype(np.float32)
    number = row[None, :, None] + BASE * (np.arange(3)[:, None, None] + 3 * np.arange(2))
    across = np.repeat(4.0 * np.sin(np.pi * number / NX) ** 2, NZ, axis=2).astype(np.float32)
    first = (lax.axis_index("gx") * lax.axis_size("gy") + lax.axis_index("gy")) * RADIX
    y_number = (first + jnp.arange(RADIX, dtype=jnp.int32)).astype(F32)
    y_wave = jnp.sin(jnp.pi * y_number / NY)
    wave = 4.0 * y_wave * y_wave
    rates = jnp.concatenate([z_rates, z_rates]).reshape(1, LANES)

    def whole(array):
        return pl.BlockSpec(array.shape, lambda q: (0,) * array.ndim)

    constants = (
        half_high,
        half_low,
        x_cos,
        x_sin,
        across,
        rates,
        twin(z_analysis.T),
        twin(z_synth),
    )
    out = pl.pallas_call(
        functools.partial(x_kernel, len(GROUPS)),
        out_shape=jax.ShapeDtypeStruct((2, RADIX, NZ, NX), F32),
        grid=(RADIX,),
        in_specs=[
            pl.BlockSpec((2 * len(pairs), BASE, LANES), lambda q: (q, 0, 0)) for pairs in GROUPS
        ]
        + [pl.BlockSpec(memory_space=pltpu.SMEM)]
        + [whole(array) for array in constants],
        out_specs=pl.BlockSpec((2, 1, NZ, NX), lambda q: (0, q, 0, 0)),
        scratch_shapes=[
            pltpu.VMEM((2 * BASE, RADIX * LANES), F32),
            pltpu.VMEM((RADIX * BASE, 2 * LANES), BF16),
            pltpu.VMEM((RADIX * BASE, 2 * LANES), BF16),
            pltpu.VMEM((2 * LANES, 2 * LANES), BF16),
            pltpu.VMEM((2 * LANES, 2 * LANES), BF16),
        ],
        compiler_params=pltpu.CompilerParams(vmem_limit_bytes=VMEM_BYTES),
    )(*arrived, wave, *constants)
    return out.transpose(0, 2, 1, 3)


def solution(mesh):
    return jax.shard_map(
        shards,
        mesh=mesh,
        in_specs=(
            P(None, BOTH),
            P(None, BOTH),
            P(BOTH),
            P(BOTH),
            P(),
            P(),
            P(),
        ),
        out_specs=P(None, None, BOTH, None),
        check_vma=False,
    )
```

```python
import math

import jax
import jax.numpy as jnp
import numpy as np
from jax import lax
from jax.experimental import pallas as pl
from jax.experimental.pallas import tpu as pltpu
from jax.sharding import PartitionSpec as P

NX = 1536
NY = 1536
WIN = 6
NZ = 64
RADIX = 6
BASE = 256
SLAB = 48
STRIP = 192
ROWS = 208
LANES = 128
UNROLL_X = 16
UNROLL_Y = 4
NODE_BLOCK = 1024
SPREAD_BLOCK = 2048
ITEMS = 36
WIDTH = 384
BOTH = ("gx", "gy")
F32 = jnp.float32
BF16 = jnp.bfloat16
HALF_ROOT3 = math.sqrt(3.0) / 2.0
VMEM_BYTES = 56 * 1024 * 1024


def split_table(table):
    high = table.astype(np.float32).astype(BF16)
    low = (table - high.astype(np.float64)).astype(np.float32).astype(BF16)
    return high, low


def base_tables():
    index = np.arange(BASE)
    angle = 2.0 * np.pi * (np.outer(index, index) % BASE) / BASE
    return np.cos(angle), np.sin(angle)


def split_value(value):
    high = value.astype(BF16)
    return high, (value - high.astype(F32)).astype(BF16)


def window(position, cell, frac):
    centred = (position - cell).astype(F32) - (WIN - 1) / 2.0
    distance = centred - frac
    inside = jnp.abs(centred) < WIN / 2.0
    return jnp.where(inside, jnp.exp(-0.5 * (distance * distance)), 0.0)


def dot_rows(left, right):
    return lax.dot_general(left, right, (((1,), (1,)), ((), ())), preferred_element_type=F32)


def matmul(left, right):
    return jnp.dot(left, right, preferred_element_type=F32)


def block_count(count_ref):
    return (count_ref[0] + (SPREAD_BLOCK - 1)) >> (SPREAD_BLOCK.bit_length() - 1)


def prepare_kernel(
    count_ref, cell_ref, frac_ref, force_ref, right_ref, z_ref, x_ref, rim_ref, left_ref, sum_ref
):
    live_count = count_ref[0]
    capacity = force_ref.shape[1]
    scale = 8.0 / math.sqrt(capacity * 256)
    sum_ref[...] = jnp.zeros_like(sum_ref)

    def body(block, carry):
        start = pl.multiple_of(block * NODE_BLOCK, NODE_BLOCK)
        span = pl.ds(start, NODE_BLOCK)

        def rows(extent):
            return lax.broadcasted_iota(jnp.int32, (extent, NODE_BLOCK), 0)

        slot = start + lax.broadcasted_iota(jnp.int32, (1, NODE_BLOCK), 1)
        amplitude = jnp.where(slot < live_count, force_ref[:, span] * scale, 0.0)
        z_part = amplitude * window(rows(NZ), cell_ref[2:3, span], frac_ref[2:3, span])
        x_part = window(rows(56), cell_ref[0:1, span], frac_ref[0:1, span])
        right = window(rows(ROWS), cell_ref[1:2, span], frac_ref[1:2, span]).astype(BF16)
        z_ref[:, span] = z_part
        x_ref[:, span] = x_part
        right_ref[:, span] = right
        for t in range(RADIX):
            left_ref[t * NZ : (t + 1) * NZ, :] = (
                z_part * x_part[SLAB + t : SLAB + t + 1, :]
            ).astype(BF16)
        sum_ref[...] += dot_rows(right, left_ref[...])
        return carry

    lax.fori_loop(0, block_count(count_ref) * (SPREAD_BLOCK // NODE_BLOCK), body, 0)
    rim_ref[...] = sum_ref[...].astype(BF16)


def spread_kernel(count_ref, right_ref, z_ref, x_ref, out_ref, left_ref, sum_ref):
    sum_ref[...] = jnp.zeros_like(sum_ref)

    def body(block, carry):
        span = pl.ds(pl.multiple_of(block * SPREAD_BLOCK, SPREAD_BLOCK), SPREAD_BLOCK)
        for pair in range(4):
            for k in range(2 * RADIX):
                x_at = pair * 2 * RADIX + k
                left_ref[k * NZ : (k + 1) * NZ, :] = (
                    z_ref[:, span] * x_ref[x_at : x_at + 1, span]
                ).astype(BF16)
            rows = slice(2 * pair * WIDTH, 2 * (pair + 1) * WIDTH)
            sum_ref[rows, :] += dot_rows(left_ref[...], right_ref[:, span])
        return carry

    lax.fori_loop(0, block_count(count_ref), body, 0)
    for j in range(8):
        out_ref[j] = sum_ref[j * WIDTH : (j + 1) * WIDTH, :].T.astype(BF16)


def rim_kernel(rim_ref, in_ref, out_ref):
    out_ref[0] = (in_ref[0].astype(F32) + rim_ref[...].astype(F32)).astype(BF16)


def y_kernel(
    in_ref, table_ref, flip_ref, cos_ref, sin_ref, out_ref, grid_ref, th_ref, tl_ref, mode_ref
):
    for j in range(8):
        grid_ref[j * STRIP : (j + 1) * STRIP, :] = in_ref[j, 0:STRIP, :].astype(F32)
    for j in range(8):
        before = (j + 7) % 8
        grid_ref[j * STRIP : j * STRIP + 16, :] += in_ref[before, STRIP:ROWS, :].astype(F32)

    def body(step, carry):
        start = pl.multiple_of(step * 16, 16)
        for p in range(3):
            lanes = slice(p * LANES, (p + 1) * LANES)
            a = [grid_ref[pl.ds(n * BASE + start, 16), lanes] for n in range(RADIX)]
            s0, s1, s2 = a[0] + a[3], a[1] + a[4], a[2] + a[5]
            d0, d1, d2 = a[0] - a[3], a[1] - a[4], a[2] - a[5]
            turned = (
                (s0 + s1 + s2, None),
                (d0 + 0.5 * (d1 - d2), -HALF_ROOT3 * (d1 + d2)),
                (s0 - 0.5 * (s1 + s2), -HALF_ROOT3 * (s1 - s2)),
                (d0 - d1 + d2, None),
            )
            for q, (real, imag) in enumerate(turned):
                if q > 0:
                    cos = cos_ref[q - 1, pl.ds(start, 16), :]
                    sin = sin_ref[q - 1, pl.ds(start, 16), :]
                    if imag is None:
                        real, imag = real * cos, -real * sin
                    else:
                        real, imag = real * cos + imag * sin, imag * cos - real * sin
                else:
                    imag = jnp.zeros_like(real)
                columns = slice(q * WIDTH + p * LANES, q * WIDTH + (p + 1) * LANES)
                for at, value in ((0, real), (BASE, imag)):
                    high, low = split_value(value)
                    th_ref[pl.ds(at + start, 16), columns] = high
                    tl_ref[pl.ds(at + start, 16), columns] = low
        return carry

    lax.fori_loop(0, BASE // 16, body, 0, unroll=UNROLL_Y)

    def put(q, part, modes, first):
        for p in range(3):
            item = (q * 2 + part) * 3 + p
            lanes = slice(first + p * LANES, first + (p + 1) * LANES)
            mode_ref[pl.ds(item, BASE, stride=ITEMS), :] = modes[:, lanes]

    for first in (1, 0, 2, 3):
        columns = slice(first * WIDTH, (first + 1) * WIDTH)
        high = th_ref[:, columns]
        low = tl_ref[:, columns]
        modes = matmul(table_ref[...], jnp.concatenate([high, high, low], axis=0))
        for part in range(2):
            rows = modes[part * BASE : (part + 1) * BASE]
            put(first, part, rows, 0)
            if first in (1, 2):
                mirror = matmul(flip_ref[...], rows.astype(BF16))
                put(RADIX - first, part, mirror if part == 0 else -mirror, 0)
    out_ref[...] = mode_ref[...].astype(BF16)


def x_kernel(
    in_ref,
    wave_ref,
    table_ref,
    cos_ref,
    sin_ref,
    across_ref,
    rate_ref,
    analysis_ref,
    synth_ref,
    out_ref,
    modes_ref,
    x_ref,
    c_ref,
    wa_ref,
    ws_ref,
):
    q = pl.program_id(0)

    @pl.when(q == 0)
    def _():
        high, low = split_value(analysis_ref[...])
        for k in range(2):
            wa_ref[k * LANES : (k + 1) * LANES, :LANES] = high
            wa_ref[k * LANES : (k + 1) * LANES, LANES:] = low
        high, low = split_value(synth_ref[...])
        for k in range(2):
            ws_ref[:LANES, k * LANES : (k + 1) * LANES] = high
            ws_ref[LANES:, k * LANES : (k + 1) * LANES] = low

    lines = jnp.concatenate([in_ref[item] for item in range(6)], axis=1)
    modes_ref[...] = matmul(table_ref[...], jnp.concatenate([lines, lines], axis=0))
    lane = lax.broadcasted_iota(jnp.int32, (16, LANES), 1)
    lower = lane < NZ
    sign = jnp.where(lower, 1.0, -1.0)
    turn_1r = jnp.where(lower, 1.0, 0.5)
    turn_2r = jnp.where(lower, 1.0, -0.5)
    turn_i = jnp.where(lower, 0.0, -HALF_ROOT3)

    def body(step, carry):
        start = pl.multiple_of(step * 16, 16)
        real, imag = [], []
        for xp in range(3):
            at_real = slice(xp * LANES, (xp + 1) * LANES)
            at_imag = slice((3 + xp) * LANES, (4 + xp) * LANES)
            mode_real = (
                modes_ref[pl.ds(start, 16), at_real] + modes_ref[pl.ds(BASE + start, 16), at_imag]
            )
            mode_imag = (
                modes_ref[pl.ds(start, 16), at_imag] - modes_ref[pl.ds(BASE + start, 16), at_real]
            )
            cos = cos_ref[xp, pl.ds(start, 16), :]
            sin = sin_ref[xp, pl.ds(start, 16), :]
            real.append(mode_real * cos + mode_imag * sin)
            imag.append(mode_imag * cos - mode_real * sin)
        sum_r, sum_i = real[1] + real[2], imag[1] + imag[2]
        dif_r, dif_i = HALF_ROOT3 * (real[1] - real[2]), HALF_ROOT3 * (imag[1] - imag[2])
        mid_r, mid_i = real[0] - 0.5 * sum_r, imag[0] - 0.5 * sum_i
        u1r, u1i = mid_r + dif_i, mid_i - dif_r
        u2r, u2i = mid_r - dif_i, mid_i + dif_r
        thirds = (
            (real[0] + sum_r, imag[0] + sum_i),
            (u1r * turn_1r - u1i * turn_i, u1i * turn_1r + u1r * turn_i),
            (u2r * turn_2r - u2i * turn_i, u2i * turn_2r + u2r * turn_i),
        )
        for m in range(3):
            for part in range(2):
                value = thirds[m][part]
                value = pltpu.roll(value, NZ, 1) + sign * value
                high, low = split_value(value)
                row = pl.ds((m * 2 + part) * BASE + start, 16)
                x_ref[row, :LANES] = high
                x_ref[row, LANES:] = low
        return carry

    lax.fori_loop(0, BASE // 16, body, 0, unroll=UNROLL_X)
    shift = rate_ref[...] + wave_ref[q]
    for m in range(3):
        inverse = 1.0 / (across_ref[m] + shift)
        for part in range(2):
            rows = slice((m * 2 + part) * BASE, (m * 2 + part + 1) * BASE)
            both = matmul(x_ref[rows, :], wa_ref[...])
            high, low = split_value((both[:, :LANES] + both[:, LANES:]) * inverse)
            c_ref[rows, :LANES] = high
            c_ref[rows, LANES:] = low
            both = dot_rows(ws_ref[...], c_ref[rows, :])
            value = both[:LANES] + both[LANES:]
            out_ref[part, 0, :, m * BASE : (m + 1) * BASE] = value[:NZ]
            out_ref[part, 0, :, (m + 3) * BASE : (m + 4) * BASE] = value[NZ:]


def vmem_call(kernel, inputs, out_shape, scratch_shapes, scalars=1, cost=None):
    specs = [pl.BlockSpec(memory_space=pltpu.SMEM)] * scalars
    specs += [pl.BlockSpec(memory_space=pltpu.VMEM)] * (len(inputs) - scalars)
    return pl.pallas_call(
        kernel,
        out_shape=out_shape,
        in_specs=specs,
        out_specs=jax.tree.map(lambda _: pl.BlockSpec(memory_space=pltpu.VMEM), out_shape),
        scratch_shapes=scratch_shapes,
        compiler_params=pltpu.CompilerParams(vmem_limit_bytes=VMEM_BYTES),
        cost_estimate=cost,
    )(*inputs)


def twin(matrix):
    zero = jnp.zeros_like(matrix)
    return jnp.concatenate(
        [jnp.concatenate([matrix, zero], axis=1), jnp.concatenate([zero, matrix], axis=1)], axis=0
    )


def shards(node_cells, node_frac, node_force, node_count, z_rates, z_synth, z_analysis):
    capacity = node_force.shape[0]
    slabs = lax.axis_size("gx")
    cos_base, sin_base = base_tables()
    full = np.block([[cos_base, sin_base], [-sin_base, cos_base]])
    high, low = split_table(full)
    y_table = np.concatenate([high, low, high], axis=1)
    flip = np.eye(BASE)[::-1].astype(BF16)
    x_table = np.concatenate(
        split_table(np.concatenate([cos_base, sin_base], axis=0)), axis=1
    )

    right, z_part, x_part, rim = vmem_call(
        prepare_kernel,
        (node_count, node_cells, node_frac, node_force.reshape(1, capacity)),
        (
            jax.ShapeDtypeStruct((ROWS, capacity), BF16),
            jax.ShapeDtypeStruct((NZ, capacity), F32),
            jax.ShapeDtypeStruct((56, capacity), F32),
            jax.ShapeDtypeStruct((ROWS, RADIX * NZ), BF16),
        ),
        [
            pltpu.VMEM((RADIX * NZ, NODE_BLOCK), BF16),
            pltpu.VMEM((ROWS, RADIX * NZ), F32),
        ],
        cost=pl.CostEstimate(flops=10**9, bytes_accessed=10**7, transcendentals=10**6),
    )
    rim = lax.ppermute(rim, "gx", [(i, (i + 1) % slabs) for i in range(slabs)])

    row = np.arange(BASE)
    angle = 2.0 * np.pi * np.outer(np.arange(1, 4), row) / NY
    y_cos = np.broadcast_to(np.cos(angle)[:, :, None], (3, BASE, LANES)).astype(np.float32)
    y_sin = np.broadcast_to(np.sin(angle)[:, :, None], (3, BASE, LANES)).astype(np.float32)

    tiles = vmem_call(
        spread_kernel,
        (node_count, right, z_part, x_part),
        jax.ShapeDtypeStruct((8, ROWS, WIDTH), BF16),
        [
            pltpu.VMEM((2 * WIDTH, SPREAD_BLOCK), BF16),
            pltpu.VMEM((8 * WIDTH, ROWS), F32),
        ],
        cost=pl.CostEstimate(flops=10**10, bytes_accessed=10**7, transcendentals=0),
    )
    tiles = pl.pallas_call(
        rim_kernel,
        out_shape=jax.ShapeDtypeStruct((8, ROWS, WIDTH), BF16),
        grid=(1,),
        in_specs=[
            pl.BlockSpec((ROWS, WIDTH), lambda i: (0, 0)),
            pl.BlockSpec((1, ROWS, WIDTH), lambda i: (0, 0, 0)),
        ],
        out_specs=pl.BlockSpec((1, ROWS, WIDTH), lambda i: (0, 0, 0)),
        input_output_aliases={1: 0},
    )(rim, tiles)
    lines = lax.all_to_all(tiles, "gy", split_axis=0, concat_axis=0, tiled=True)
    spectrum = vmem_call(
        y_kernel,
        (lines, y_table, flip, y_cos, y_sin),
        jax.ShapeDtypeStruct((BASE * ITEMS, LANES), BF16),
        [
            pltpu.VMEM((NY, WIDTH), F32),
            pltpu.VMEM((2 * BASE, 4 * WIDTH), BF16),
            pltpu.VMEM((2 * BASE, 4 * WIDTH), BF16),
            pltpu.VMEM((BASE * ITEMS, LANES), F32),
        ],
        scalars=0,
        cost=pl.CostEstimate(flops=5 * 10**9, bytes_accessed=10**7, transcendentals=0),
    )
    packed = spectrum.reshape(BASE, ITEMS // 4, 4, LANES)
    moved = lax.all_to_all(packed, BOTH, split_axis=0, concat_axis=0, tiled=True)
    arrived = moved.transpose(1, 2, 0, 3).reshape(ITEMS, BASE, LANES)

    offset = np.arange(RADIX).reshape(3, 2)
    angle = 2.0 * np.pi * offset[:, None, :] * row[None, :, None] / NX
    x_cos = np.repeat(np.cos(angle), NZ, axis=2).astype(np.float32)
    x_sin = np.repeat(np.sin(angle), NZ, axis=2).astype(np.float32)
    number = row[None, :, None] + BASE * (np.arange(3)[:, None, None] + 3 * np.arange(2))
    across = np.repeat(4.0 * np.sin(np.pi * number / NX) ** 2, NZ, axis=2).astype(np.float32)
    first = (lax.axis_index("gx") * lax.axis_size("gy") + lax.axis_index("gy")) * RADIX
    y_number = (first + jnp.arange(RADIX, dtype=jnp.int32)).astype(F32)
    y_wave = jnp.sin(jnp.pi * y_number / NY)
    wave = 4.0 * y_wave * y_wave
    rates = jnp.concatenate([z_rates, z_rates]).reshape(1, LANES)

    def whole(array):
        return pl.BlockSpec(array.shape, lambda q: (0,) * array.ndim)

    constants = (
        x_table,
        x_cos,
        x_sin,
        across,
        rates,
        twin(z_analysis.T),
        twin(z_synth),
    )
    out = pl.pallas_call(
        x_kernel,
        out_shape=jax.ShapeDtypeStruct((2, RADIX, NZ, NX), F32),
        grid=(RADIX,),
        in_specs=[pl.BlockSpec((6, BASE, LANES), lambda q: (q, 0, 0))]
        + [pl.BlockSpec(memory_space=pltpu.SMEM)]
        + [whole(array) for array in constants],
        out_specs=pl.BlockSpec((2, 1, NZ, NX), lambda q: (0, q, 0, 0)),
        scratch_shapes=[
            pltpu.VMEM((2 * BASE, RADIX * LANES), F32),
            pltpu.VMEM((RADIX * BASE, 2 * LANES), BF16),
            pltpu.VMEM((RADIX * BASE, 2 * LANES), BF16),
            pltpu.VMEM((2 * LANES, 2 * LANES), BF16),
            pltpu.VMEM((2 * LANES, 2 * LANES), BF16),
        ],
        compiler_params=pltpu.CompilerParams(vmem_limit_bytes=VMEM_BYTES),
    )(arrived, wave, *constants)
    return out.transpose(0, 2, 1, 3)


def solution(mesh):
    return jax.shard_map(
        shards,
        mesh=mesh,
        in_specs=(
            P(None, BOTH),
            P(None, BOTH),
            P(BOTH),
            P(BOTH),
            P(),
            P(),
            P(),
        ),
        out_specs=P(None, None, BOTH, None),
        check_vma=False,
    )
```

```python
import itertools
import math

import jax
import jax.numpy as jnp
import numpy as np
from jax import lax
from jax.experimental import pallas as pl
from jax.experimental.pallas import tpu as pltpu
from jax.sharding import PartitionSpec as P

NX = 1536
NY = 1536
WIN = 6
NZ = 64
RADIX = 6
BASE = 256
SLAB = 48
STRIP = 192
ROWS = 208
LANES = 128
UNROLL_X = 16
UNROLL_Y = 4
NODE_BLOCK = 1024
SPREAD_BLOCK = 2048
ITEMS = 36
WIDTH = 384
BOTH = ("gx", "gy")
TURNS = tuple((dx, way) for dx in range(4) for way in range(2))
F32 = jnp.float32
BF16 = jnp.bfloat16
HALF_ROOT3 = math.sqrt(3.0) / 2.0
MIB = 1024 * 1024
PREPARE_BYTES = 14 * MIB
SPREAD_BYTES = 20 * MIB
SORT_BYTES = 8 * MIB
Y_BYTES = 26 * MIB
X_BYTES = 26 * MIB


def split_table(table):
    high = table.astype(np.float32).astype(BF16)
    low = (table - high.astype(np.float64)).astype(np.float32).astype(BF16)
    return high, low


def base_tables():
    index = np.arange(BASE)
    angle = 2.0 * np.pi * (np.outer(index, index) % BASE) / BASE
    return np.cos(angle), np.sin(angle)


def split_value(value):
    high = value.astype(BF16)
    return high, (value - high.astype(F32)).astype(BF16)


def window(position, cell, frac):
    centred = (position - cell).astype(F32) - (WIN - 1) / 2.0
    distance = centred - frac
    inside = jnp.abs(centred) < WIN / 2.0
    return jnp.where(inside, jnp.exp(-0.5 * (distance * distance)), 0.0)


def dot_rows(left, right):
    return lax.dot_general(left, right, (((1,), (1,)), ((), ())), preferred_element_type=F32)


def matmul(left, right):
    return jnp.dot(left, right, preferred_element_type=F32)


def block_count(count_ref):
    return (count_ref[0] + (SPREAD_BLOCK - 1)) >> (SPREAD_BLOCK.bit_length() - 1)


def prepare_kernel(
    count_ref, cell_ref, frac_ref, force_ref, right_ref, z_ref, x_ref, rim_ref, left_ref, sum_ref
):
    live_count = count_ref[0]
    capacity = force_ref.shape[1]
    scale = 8.0 / math.sqrt(capacity * 256)
    sum_ref[...] = jnp.zeros_like(sum_ref)

    def body(block, carry):
        start = pl.multiple_of(block * NODE_BLOCK, NODE_BLOCK)
        span = pl.ds(start, NODE_BLOCK)

        def rows(extent):
            return lax.broadcasted_iota(jnp.int32, (extent, NODE_BLOCK), 0)

        slot = start + lax.broadcasted_iota(jnp.int32, (1, NODE_BLOCK), 1)
        amplitude = jnp.where(slot < live_count, force_ref[:, span] * scale, 0.0)
        z_part = amplitude * window(rows(NZ), cell_ref[2:3, span], frac_ref[2:3, span])
        x_part = window(rows(56), cell_ref[0:1, span], frac_ref[0:1, span])
        right = window(rows(ROWS), cell_ref[1:2, span], frac_ref[1:2, span]).astype(BF16)
        z_ref[:, span] = z_part
        x_ref[:, span] = x_part
        right_ref[:, span] = right
        for t in range(RADIX):
            left_ref[t * NZ : (t + 1) * NZ, :] = (
                z_part * x_part[SLAB + t : SLAB + t + 1, :]
            ).astype(BF16)
        sum_ref[...] += dot_rows(right, left_ref[...])
        return carry

    lax.fori_loop(0, block_count(count_ref) * (SPREAD_BLOCK // NODE_BLOCK), body, 0)
    rim_ref[...] = sum_ref[...].astype(BF16)


def spread_kernel(count_ref, right_ref, z_ref, x_ref, out_ref, left_ref, sum_ref):
    sum_ref[...] = jnp.zeros_like(sum_ref)

    def body(block, carry):
        span = pl.ds(pl.multiple_of(block * SPREAD_BLOCK, SPREAD_BLOCK), SPREAD_BLOCK)
        for pair in range(4):
            for k in range(2 * RADIX):
                x_at = pair * 2 * RADIX + k
                left_ref[k * NZ : (k + 1) * NZ, :] = (
                    z_ref[:, span] * x_ref[x_at : x_at + 1, span]
                ).astype(BF16)
            rows = slice(2 * pair * WIDTH, 2 * (pair + 1) * WIDTH)
            sum_ref[rows, :] += dot_rows(left_ref[...], right_ref[:, span])
        return carry

    lax.fori_loop(0, block_count(count_ref), body, 0)
    for j in range(8):
        out_ref[j] = sum_ref[j * WIDTH : (j + 1) * WIDTH, :].T.astype(BF16)


def partner(turn, sign):
    dx, way = TURNS[turn]
    gx, gy = lax.axis_index("gx"), lax.axis_index("gy")
    dz = 2 - 4 * ((gx + way) & 1)
    x_at = ((gy >> 1) + sign * dx) & 3
    z_at = ((gy & 1) * 4 + (gx >> 3) + sign * dz) & 7
    return x_at * 2 + (z_at >> 2)


def sort_kernel(in_ref, rim_ref, *out_refs):
    for turn, out_ref in enumerate(out_refs):
        block = partner(turn, 1)
        rim = jnp.where(block == 0, rim_ref[...].astype(F32), 0.0)
        out_ref[...] = (in_ref[block].astype(F32) + rim).astype(BF16)


def y_kernel(*refs):
    in_refs = refs[:8]
    table_ref, flip_ref, cos_ref, sin_ref, out_ref, grid_ref, th_ref, tl_ref, mode_ref = refs[8:]
    for turn in range(8):
        start = pl.multiple_of(partner(turn, -1) * STRIP, STRIP)
        grid_ref[pl.ds(start, STRIP), :] = in_refs[turn][0:STRIP, :].astype(F32)
    for turn in range(8):
        start = pl.multiple_of(((partner(turn, -1) + 1) & 7) * STRIP, STRIP)
        grid_ref[pl.ds(start, 16), :] += in_refs[turn][STRIP:ROWS, :].astype(F32)

    def body(step, carry):
        start = pl.multiple_of(step * 16, 16)
        for p in range(3):
            lanes = slice(p * LANES, (p + 1) * LANES)
            a = [grid_ref[pl.ds(n * BASE + start, 16), lanes] for n in range(RADIX)]
            s0, s1, s2 = a[0] + a[3], a[1] + a[4], a[2] + a[5]
            d0, d1, d2 = a[0] - a[3], a[1] - a[4], a[2] - a[5]
            turned = (
                (s0 + s1 + s2, None),
                (d0 + 0.5 * (d1 - d2), -HALF_ROOT3 * (d1 + d2)),
                (s0 - 0.5 * (s1 + s2), -HALF_ROOT3 * (s1 - s2)),
                (d0 - d1 + d2, None),
            )
            for q, (real, imag) in enumerate(turned):
                if q > 0:
                    cos = cos_ref[q - 1, pl.ds(start, 16), :]
                    sin = sin_ref[q - 1, pl.ds(start, 16), :]
                    if imag is None:
                        real, imag = real * cos, -real * sin
                    else:
                        real, imag = real * cos + imag * sin, imag * cos - real * sin
                else:
                    imag = jnp.zeros_like(real)
                columns = slice(q * WIDTH + p * LANES, q * WIDTH + (p + 1) * LANES)
                for at, value in ((0, real), (BASE, imag)):
                    high, low = split_value(value)
                    th_ref[pl.ds(at + start, 16), columns] = high
                    tl_ref[pl.ds(at + start, 16), columns] = low
        return carry

    lax.fori_loop(0, BASE // 16, body, 0, unroll=UNROLL_Y)

    def put(q, part, modes, first):
        for p in range(3):
            item = (q * 2 + part) * 3 + p
            lanes = slice(first + p * LANES, first + (p + 1) * LANES)
            mode_ref[pl.ds(item, BASE, stride=ITEMS), :] = modes[:, lanes]

    for first in (1, 0, 2, 3):
        columns = slice(first * WIDTH, (first + 1) * WIDTH)
        high = th_ref[:, columns]
        low = tl_ref[:, columns]
        modes = matmul(table_ref[...], jnp.concatenate([high, high, low], axis=0))
        for part in range(2):
            rows = modes[part * BASE : (part + 1) * BASE]
            put(first, part, rows, 0)
            if first in (1, 2):
                mirror = matmul(flip_ref[...], rows.astype(BF16))
                put(RADIX - first, part, mirror if part == 0 else -mirror, 0)
    out_ref[...] = mode_ref[...].astype(BF16)


def x_kernel(
    in_ref,
    wave_ref,
    table_ref,
    cos_ref,
    sin_ref,
    across_ref,
    rate_ref,
    analysis_ref,
    synth_ref,
    out_ref,
    modes_ref,
    x_ref,
    c_ref,
    wa_ref,
    ws_ref,
):
    q = pl.program_id(0)

    @pl.when(q == 0)
    def _():
        high, low = split_value(analysis_ref[...])
        for k in range(2):
            wa_ref[k * LANES : (k + 1) * LANES, :LANES] = high
            wa_ref[k * LANES : (k + 1) * LANES, LANES:] = low
        high, low = split_value(synth_ref[...])
        for k in range(2):
            ws_ref[:LANES, k * LANES : (k + 1) * LANES] = high
            ws_ref[LANES:, k * LANES : (k + 1) * LANES] = low

    lines = jnp.concatenate([in_ref[item] for item in range(6)], axis=1)
    modes_ref[...] = matmul(table_ref[...], jnp.concatenate([lines, lines], axis=0))
    lane = lax.broadcasted_iota(jnp.int32, (16, LANES), 1)
    lower = lane < NZ
    sign = jnp.where(lower, 1.0, -1.0)
    turn_1r = jnp.where(lower, 1.0, 0.5)
    turn_2r = jnp.where(lower, 1.0, -0.5)
    turn_i = jnp.where(lower, 0.0, -HALF_ROOT3)

    def body(step, carry):
        start = pl.multiple_of(step * 16, 16)
        real, imag = [], []
        for xp in range(3):
            at_real = slice(xp * LANES, (xp + 1) * LANES)
            at_imag = slice((3 + xp) * LANES, (4 + xp) * LANES)
            mode_real = (
                modes_ref[pl.ds(start, 16), at_real] + modes_ref[pl.ds(BASE + start, 16), at_imag]
            )
            mode_imag = (
                modes_ref[pl.ds(start, 16), at_imag] - modes_ref[pl.ds(BASE + start, 16), at_real]
            )
            cos = cos_ref[xp, pl.ds(start, 16), :]
            sin = sin_ref[xp, pl.ds(start, 16), :]
            real.append(mode_real * cos + mode_imag * sin)
            imag.append(mode_imag * cos - mode_real * sin)
        sum_r, sum_i = real[1] + real[2], imag[1] + imag[2]
        dif_r, dif_i = HALF_ROOT3 * (real[1] - real[2]), HALF_ROOT3 * (imag[1] - imag[2])
        mid_r, mid_i = real[0] - 0.5 * sum_r, imag[0] - 0.5 * sum_i
        u1r, u1i = mid_r + dif_i, mid_i - dif_r
        u2r, u2i = mid_r - dif_i, mid_i + dif_r
        thirds = (
            (real[0] + sum_r, imag[0] + sum_i),
            (u1r * turn_1r - u1i * turn_i, u1i * turn_1r + u1r * turn_i),
            (u2r * turn_2r - u2i * turn_i, u2i * turn_2r + u2r * turn_i),
        )
        for m in range(3):
            for part in range(2):
                value = thirds[m][part]
                value = pltpu.roll(value, NZ, 1) + sign * value
                high, low = split_value(value)
                row = pl.ds((m * 2 + part) * BASE + start, 16)
                x_ref[row, :LANES] = high
                x_ref[row, LANES:] = low
        return carry

    lax.fori_loop(0, BASE // 16, body, 0, unroll=UNROLL_X)
    shift = rate_ref[...] + wave_ref[q]
    both = matmul(x_ref[...], wa_ref[...])
    for m in range(3):
        inverse = 1.0 / (across_ref[m] + shift)
        for part in range(2):
            rows = slice((m * 2 + part) * BASE, (m * 2 + part + 1) * BASE)
            high, low = split_value((both[rows, :LANES] + both[rows, LANES:]) * inverse)
            c_ref[rows, :LANES] = high
            c_ref[rows, LANES:] = low
    both = dot_rows(ws_ref[...], c_ref[...])
    value = both[:LANES] + both[LANES:]
    for m in range(3):
        for part in range(2):
            columns = slice((m * 2 + part) * BASE, (m * 2 + part + 1) * BASE)
            out_ref[part, 0, :, m * BASE : (m + 1) * BASE] = value[:NZ, columns]
            out_ref[part, 0, :, (m + 3) * BASE : (m + 4) * BASE] = value[NZ:, columns]


def vmem_call(kernel, inputs, out_shape, scratch_shapes, limit, scalars=1, cost=None):
    specs = [pl.BlockSpec(memory_space=pltpu.SMEM)] * scalars
    specs += [pl.BlockSpec(memory_space=pltpu.VMEM)] * (len(inputs) - scalars)
    return pl.pallas_call(
        kernel,
        out_shape=out_shape,
        in_specs=specs,
        out_specs=jax.tree.map(lambda _: pl.BlockSpec(memory_space=pltpu.VMEM), out_shape),
        scratch_shapes=scratch_shapes,
        compiler_params=pltpu.CompilerParams(vmem_limit_bytes=limit),
        cost_estimate=cost,
    )(*inputs)


def place(x, y, z, core):
    return ((z % 4 * 8 + y * 2 + core) * 8) + x * 2 + z // 4


def turn_route(dx, way):
    return [
        (place(x, y, z, core), place((x + dx) % 4, y, (z + 2 - 4 * ((core + way) % 2)) % 8, core))
        for x, y, z, core in itertools.product(range(4), range(4), range(8), range(2))
    ]


def twin(matrix):
    zero = jnp.zeros_like(matrix)
    return jnp.concatenate(
        [jnp.concatenate([matrix, zero], axis=1), jnp.concatenate([zero, matrix], axis=1)], axis=0
    )


def shards(node_cells, node_frac, node_force, node_count, z_rates, z_synth, z_analysis):
    capacity = node_force.shape[0]
    slabs = lax.axis_size("gx")
    cos_base, sin_base = base_tables()
    full = np.block([[cos_base, sin_base], [-sin_base, cos_base]])
    high, low = split_table(full)
    y_table = np.concatenate([high, low, high], axis=1)
    flip = np.eye(BASE)[::-1].astype(BF16)
    order = np.arange(BASE) ^ (BASE // 2)
    x_table = np.concatenate(
        split_table(np.concatenate([cos_base, sin_base], axis=0)[:, order]), axis=1
    )

    right, z_part, x_part, rim = vmem_call(
        prepare_kernel,
        (node_count, node_cells, node_frac, node_force.reshape(1, capacity)),
        (
            jax.ShapeDtypeStruct((ROWS, capacity), BF16),
            jax.ShapeDtypeStruct((NZ, capacity), F32),
            jax.ShapeDtypeStruct((56, capacity), F32),
            jax.ShapeDtypeStruct((ROWS, RADIX * NZ), BF16),
        ),
        [
            pltpu.VMEM((RADIX * NZ, NODE_BLOCK), BF16),
            pltpu.VMEM((ROWS, RADIX * NZ), F32),
        ],
        PREPARE_BYTES,
        cost=pl.CostEstimate(flops=10**9, bytes_accessed=10**7, transcendentals=10**6),
    )
    rim = lax.ppermute(rim, "gx", [(i, (i + 1) % slabs) for i in range(slabs)])

    row = np.arange(BASE)
    angle = 2.0 * np.pi * np.outer(np.arange(1, 4), row) / NY
    y_cos = np.broadcast_to(np.cos(angle)[:, :, None], (3, BASE, LANES)).astype(np.float32)
    y_sin = np.broadcast_to(np.sin(angle)[:, :, None], (3, BASE, LANES)).astype(np.float32)

    tiles = vmem_call(
        spread_kernel,
        (node_count, right, z_part, x_part),
        jax.ShapeDtypeStruct((8, ROWS, WIDTH), BF16),
        [
            pltpu.VMEM((2 * WIDTH, SPREAD_BLOCK), BF16),
            pltpu.VMEM((8 * WIDTH, ROWS), F32),
        ],
        SPREAD_BYTES,
        cost=pl.CostEstimate(flops=10**10, bytes_accessed=10**7, transcendentals=0),
    )
    line = jax.ShapeDtypeStruct((ROWS, WIDTH), BF16)
    parts = vmem_call(sort_kernel, (tiles, rim), (line,) * 8, [], scalars=0, limit=SORT_BYTES)
    lines = [
        lax.ppermute(part, BOTH, turn_route(dx, way)) for part, (dx, way) in zip(parts, TURNS)
    ]
    spectrum = vmem_call(
        y_kernel,
        (*lines, y_table, flip, y_cos, y_sin),
        jax.ShapeDtypeStruct((BASE * ITEMS, LANES), BF16),
        [
            pltpu.VMEM((NY, WIDTH), F32),
            pltpu.VMEM((2 * BASE, 4 * WIDTH), BF16),
            pltpu.VMEM((2 * BASE, 4 * WIDTH), BF16),
            pltpu.VMEM((BASE * ITEMS, LANES), F32),
        ],
        Y_BYTES,
        scalars=0,
        cost=pl.CostEstimate(flops=5 * 10**9, bytes_accessed=10**7, transcendentals=0),
    )
    packed = spectrum.reshape(BASE, ITEMS // 4, 4, LANES)
    moved = lax.all_to_all(packed, BOTH, split_axis=0, concat_axis=0, tiled=True)
    arrived = moved.transpose(1, 2, 0, 3).reshape(ITEMS, BASE, LANES)

    offset = np.arange(RADIX).reshape(3, 2)
    angle = 2.0 * np.pi * offset[:, None, :] * row[None, :, None] / NX
    x_cos = np.repeat(np.cos(angle), NZ, axis=2).astype(np.float32)
    x_sin = np.repeat(np.sin(angle), NZ, axis=2).astype(np.float32)
    number = row[None, :, None] + BASE * (np.arange(3)[:, None, None] + 3 * np.arange(2))
    across = np.repeat(4.0 * np.sin(np.pi * number / NX) ** 2, NZ, axis=2).astype(np.float32)
    first = (lax.axis_index("gx") * lax.axis_size("gy") + lax.axis_index("gy")) * RADIX
    y_number = (first + jnp.arange(RADIX, dtype=jnp.int32)).astype(F32)
    y_wave = jnp.sin(jnp.pi * y_number / NY)
    wave = 4.0 * y_wave * y_wave
    rates = jnp.concatenate([z_rates, z_rates]).reshape(1, LANES)

    def whole(array):
        return pl.BlockSpec(array.shape, lambda q: (0,) * array.ndim)

    constants = (
        x_table,
        x_cos,
        x_sin,
        across,
        rates,
        twin(z_analysis.T),
        twin(z_synth),
    )
    out = pl.pallas_call(
        x_kernel,
        out_shape=jax.ShapeDtypeStruct((2, RADIX, NZ, NX), F32),
        grid=(RADIX,),
        in_specs=[pl.BlockSpec((6, BASE, LANES), lambda q: (q, 0, 0))]
        + [pl.BlockSpec(memory_space=pltpu.SMEM)]
        + [whole(array) for array in constants],
        out_specs=pl.BlockSpec((2, 1, NZ, NX), lambda q: (0, q, 0, 0)),
        scratch_shapes=[
            pltpu.VMEM((2 * BASE, RADIX * LANES), F32),
            pltpu.VMEM((RADIX * BASE, 2 * LANES), BF16),
            pltpu.VMEM((RADIX * BASE, 2 * LANES), BF16),
            pltpu.VMEM((2 * LANES, 2 * LANES), BF16),
            pltpu.VMEM((2 * LANES, 2 * LANES), BF16),
        ],
        compiler_params=pltpu.CompilerParams(vmem_limit_bytes=X_BYTES),
    )(arrived, wave, *constants)
    return out.transpose(0, 2, 1, 3)


def solution(mesh):
    return jax.shard_map(
        shards,
        mesh=mesh,
        in_specs=(
            P(None, BOTH),
            P(None, BOTH),
            P(BOTH),
            P(BOTH),
            P(),
            P(),
            P(),
        ),
        out_specs=P(None, None, BOTH, None),
        check_vma=False,
    )
```

```python
import itertools
import math

import jax
import jax.numpy as jnp
import numpy as np
from jax import lax
from jax.experimental import pallas as pl
from jax.experimental.pallas import tpu as pltpu
from jax.sharding import PartitionSpec as P

NX = 1536
NY = 1536
WIN = 6
NZ = 64
RADIX = 6
BASE = 256
SLAB = 48
STRIP = 192
ROWS = 208
LANES = 128
UNROLL_X = 16
UNROLL_Y = 4
NODE_BLOCK = 1024
SPREAD_BLOCK = 2048
ITEMS = 36
WIDTH = 384
BOTH = ("gx", "gy")
TURNS = tuple((dx, way) for dx in range(4) for way in range(2))
F32 = jnp.float32
BF16 = jnp.bfloat16
HALF_ROOT3 = math.sqrt(3.0) / 2.0
MIB = 1024 * 1024
PREPARE_BYTES = 14 * MIB
SPREAD_BYTES = 20 * MIB
SORT_BYTES = 8 * MIB
Y_BYTES = 26 * MIB
X_BYTES = 26 * MIB


def split_table(table):
    high = table.astype(np.float32).astype(BF16)
    low = (table - high.astype(np.float64)).astype(np.float32).astype(BF16)
    return high, low


def base_tables():
    index = np.arange(BASE)
    angle = 2.0 * np.pi * (np.outer(index, index) % BASE) / BASE
    return np.cos(angle), np.sin(angle)


def split_value(value):
    high = value.astype(BF16)
    return high, (value - high.astype(F32)).astype(BF16)


def window(position, cell, frac):
    centred = (position - cell).astype(F32) - (WIN - 1) / 2.0
    distance = centred - frac
    inside = jnp.abs(centred) < WIN / 2.0
    return jnp.where(inside, jnp.exp(-0.5 * (distance * distance)), 0.0)


def dot_rows(left, right):
    return lax.dot_general(left, right, (((1,), (1,)), ((), ())), preferred_element_type=F32)


def matmul(left, right):
    return jnp.dot(left, right, preferred_element_type=F32)


def block_count(count_ref):
    return (count_ref[0] + (SPREAD_BLOCK - 1)) >> (SPREAD_BLOCK.bit_length() - 1)


def prepare_kernel(
    count_ref,
    cell_in,
    frac_in,
    force_in,
    right_ref,
    z_ref,
    x_ref,
    rim_ref,
    cell_ref,
    frac_ref,
    force_ref,
    left_ref,
    sum_ref,
    arrival,
):
    copies = [
        pltpu.make_async_copy(source, target, arrival.at[at])
        for at, (source, target) in enumerate(
            ((cell_in, cell_ref), (frac_in, frac_ref), (force_in, force_ref))
        )
    ]
    for copy in copies:
        copy.start()
    live_count = count_ref[0]
    capacity = force_ref.shape[1]
    scale = 8.0 / math.sqrt(capacity * 256)
    sum_ref[...] = jnp.zeros_like(sum_ref)
    for copy in copies:
        copy.wait()

    def body(block, carry):
        start = pl.multiple_of(block * NODE_BLOCK, NODE_BLOCK)
        span = pl.ds(start, NODE_BLOCK)

        def rows(extent):
            return lax.broadcasted_iota(jnp.int32, (extent, NODE_BLOCK), 0)

        slot = start + lax.broadcasted_iota(jnp.int32, (1, NODE_BLOCK), 1)
        amplitude = jnp.where(slot < live_count, force_ref[:, span] * scale, 0.0)
        z_part = amplitude * window(rows(NZ), cell_ref[2:3, span], frac_ref[2:3, span])
        x_part = window(rows(56), cell_ref[0:1, span], frac_ref[0:1, span])
        right = window(rows(ROWS), cell_ref[1:2, span], frac_ref[1:2, span]).astype(BF16)
        z_ref[:, span] = z_part
        x_ref[:, span] = x_part
        right_ref[:, span] = right
        for t in range(RADIX):
            left_ref[t * NZ : (t + 1) * NZ, :] = (
                z_part * x_part[SLAB + t : SLAB + t + 1, :]
            ).astype(BF16)
        sum_ref[...] += dot_rows(right, left_ref[...])
        return carry

    lax.fori_loop(0, block_count(count_ref) * (SPREAD_BLOCK // NODE_BLOCK), body, 0)
    rim_ref[...] = sum_ref[...].astype(BF16)


def spread_kernel(count_ref, right_ref, z_ref, x_ref, out_ref, left_ref, sum_ref):
    sum_ref[...] = jnp.zeros_like(sum_ref)

    def body(block, carry):
        span = pl.ds(pl.multiple_of(block * SPREAD_BLOCK, SPREAD_BLOCK), SPREAD_BLOCK)
        for pair in range(4):
            for k in range(2 * RADIX):
                x_at = pair * 2 * RADIX + k
                left_ref[k * NZ : (k + 1) * NZ, :] = (
                    z_ref[:, span] * x_ref[x_at : x_at + 1, span]
                ).astype(BF16)
            rows = slice(2 * pair * WIDTH, 2 * (pair + 1) * WIDTH)
            sum_ref[rows, :] += dot_rows(left_ref[...], right_ref[:, span])
        return carry

    lax.fori_loop(0, block_count(count_ref), body, 0)
    for j in range(8):
        out_ref[j] = sum_ref[j * WIDTH : (j + 1) * WIDTH, :].T.astype(BF16)


def partner(turn, sign):
    dx, way = TURNS[turn]
    gx, gy = lax.axis_index("gx"), lax.axis_index("gy")
    dz = 2 - 4 * ((gx + way) & 1)
    x_at = ((gy >> 1) + sign * dx) & 3
    z_at = ((gy & 1) * 4 + (gx >> 3) + sign * dz) & 7
    return x_at * 2 + (z_at >> 2)


def sort_kernel(in_ref, rim_ref, *out_refs):
    for turn, out_ref in enumerate(out_refs):
        block = partner(turn, 1)
        rim = jnp.where(block == 0, rim_ref[...].astype(F32), 0.0)
        out_ref[...] = (in_ref[block].astype(F32) + rim).astype(BF16)


def y_kernel(*refs):
    in_refs = refs[:8]
    table_ref, flip_ref, cos_ref, sin_ref, out_ref, grid_ref, th_ref, mode_ref = refs[8:]
    for turn in range(8):
        start = pl.multiple_of(partner(turn, -1) * STRIP, STRIP)
        grid_ref[pl.ds(start, STRIP), :] = in_refs[turn][0:STRIP, :].astype(F32)
    for turn in range(8):
        start = pl.multiple_of(((partner(turn, -1) + 1) & 7) * STRIP, STRIP)
        grid_ref[pl.ds(start, 16), :] += in_refs[turn][STRIP:ROWS, :].astype(F32)

    def body(step, carry):
        start = pl.multiple_of(step * 16, 16)
        for p in range(3):
            lanes = slice(p * LANES, (p + 1) * LANES)
            a = [grid_ref[pl.ds(n * BASE + start, 16), lanes] for n in range(RADIX)]
            s0, s1, s2 = a[0] + a[3], a[1] + a[4], a[2] + a[5]
            d0, d1, d2 = a[0] - a[3], a[1] - a[4], a[2] - a[5]
            turned = (
                (s0 + s1 + s2, None),
                (d0 + 0.5 * (d1 - d2), -HALF_ROOT3 * (d1 + d2)),
                (s0 - 0.5 * (s1 + s2), -HALF_ROOT3 * (s1 - s2)),
                (d0 - d1 + d2, None),
            )
            for q, (real, imag) in enumerate(turned):
                if q > 0:
                    cos = cos_ref[q - 1, pl.ds(start, 16), :]
                    sin = sin_ref[q - 1, pl.ds(start, 16), :]
                    if imag is None:
                        real, imag = real * cos, -real * sin
                    else:
                        real, imag = real * cos + imag * sin, imag * cos - real * sin
                else:
                    imag = jnp.zeros_like(real)
                columns = slice(q * WIDTH + p * LANES, q * WIDTH + (p + 1) * LANES)
                for at, value in ((0, real), (BASE, imag)):
                    th_ref[pl.ds(at + start, 16), columns] = value.astype(BF16)
        return carry

    lax.fori_loop(0, BASE // 16, body, 0, unroll=UNROLL_Y)

    def put(q, part, modes, first):
        for p in range(3):
            item = (q * 2 + part) * 3 + p
            lanes = slice(first + p * LANES, first + (p + 1) * LANES)
            mode_ref[pl.ds(item, BASE, stride=ITEMS), :] = modes[:, lanes]

    for first in (1, 0, 2, 3):
        columns = slice(first * WIDTH, (first + 1) * WIDTH)
        high = th_ref[:, columns]
        modes = matmul(table_ref[...], high)
        for part in range(2):
            rows = modes[part * BASE : (part + 1) * BASE]
            put(first, part, rows, 0)
            if first in (1, 2):
                mirror = matmul(flip_ref[...], rows.astype(BF16))
                put(RADIX - first, part, mirror if part == 0 else -mirror, 0)
    out_ref[...] = mode_ref[...].astype(BF16)


def x_kernel(
    in_ref,
    wave_ref,
    table_ref,
    cos_ref,
    sin_ref,
    across_ref,
    rate_ref,
    analysis_ref,
    synth_ref,
    out_ref,
    modes_ref,
    x_ref,
    c_ref,
    wa_ref,
    ws_ref,
):
    q = pl.program_id(0)

    @pl.when(q == 0)
    def _():
        high, low = split_value(analysis_ref[...])
        for k in range(2):
            wa_ref[k * LANES : (k + 1) * LANES, :LANES] = high
            wa_ref[k * LANES : (k + 1) * LANES, LANES:] = low
        high, low = split_value(synth_ref[...])
        for k in range(2):
            ws_ref[:LANES, k * LANES : (k + 1) * LANES] = high
            ws_ref[LANES:, k * LANES : (k + 1) * LANES] = low

    lines = jnp.concatenate([in_ref[item] for item in range(6)], axis=1)
    modes_ref[...] = matmul(table_ref[...], lines)
    lane = lax.broadcasted_iota(jnp.int32, (16, LANES), 1)
    lower = lane < NZ
    sign = jnp.where(lower, 1.0, -1.0)
    turn_1r = jnp.where(lower, 1.0, 0.5)
    turn_2r = jnp.where(lower, 1.0, -0.5)
    turn_i = jnp.where(lower, 0.0, -HALF_ROOT3)

    def body(step, carry):
        start = pl.multiple_of(step * 16, 16)
        real, imag = [], []
        for xp in range(3):
            at_real = slice(xp * LANES, (xp + 1) * LANES)
            at_imag = slice((3 + xp) * LANES, (4 + xp) * LANES)
            mode_real = (
                modes_ref[pl.ds(start, 16), at_real] + modes_ref[pl.ds(BASE + start, 16), at_imag]
            )
            mode_imag = (
                modes_ref[pl.ds(start, 16), at_imag] - modes_ref[pl.ds(BASE + start, 16), at_real]
            )
            cos = cos_ref[xp, pl.ds(start, 16), :]
            sin = sin_ref[xp, pl.ds(start, 16), :]
            real.append(mode_real * cos + mode_imag * sin)
            imag.append(mode_imag * cos - mode_real * sin)
        sum_r, sum_i = real[1] + real[2], imag[1] + imag[2]
        dif_r, dif_i = HALF_ROOT3 * (real[1] - real[2]), HALF_ROOT3 * (imag[1] - imag[2])
        mid_r, mid_i = real[0] - 0.5 * sum_r, imag[0] - 0.5 * sum_i
        u1r, u1i = mid_r + dif_i, mid_i - dif_r
        u2r, u2i = mid_r - dif_i, mid_i + dif_r
        thirds = (
            (real[0] + sum_r, imag[0] + sum_i),
            (u1r * turn_1r - u1i * turn_i, u1i * turn_1r + u1r * turn_i),
            (u2r * turn_2r - u2i * turn_i, u2i * turn_2r + u2r * turn_i),
        )
        for m in range(3):
            for part in range(2):
                value = thirds[m][part]
                value = pltpu.roll(value, NZ, 1) + sign * value
                high, low = split_value(value)
                row = pl.ds((m * 2 + part) * BASE + start, 16)
                x_ref[row, :LANES] = high
                x_ref[row, LANES:] = low
        return carry

    lax.fori_loop(0, BASE // 16, body, 0, unroll=UNROLL_X)
    shift = rate_ref[...] + wave_ref[q]
    both = matmul(x_ref[...], wa_ref[...])
    for m in range(3):
        inverse = 1.0 / (across_ref[m] + shift)
        for part in range(2):
            rows = slice((m * 2 + part) * BASE, (m * 2 + part + 1) * BASE)
            high, low = split_value((both[rows, :LANES] + both[rows, LANES:]) * inverse)
            c_ref[rows, :LANES] = high
            c_ref[rows, LANES:] = low
    both = dot_rows(ws_ref[...], c_ref[...])
    value = both[:LANES] + both[LANES:]
    for m in range(3):
        for part in range(2):
            columns = slice((m * 2 + part) * BASE, (m * 2 + part + 1) * BASE)
            out_ref[part, 0, :, m * BASE : (m + 1) * BASE] = value[:NZ, columns]
            out_ref[part, 0, :, (m + 3) * BASE : (m + 4) * BASE] = value[NZ:, columns]


def vmem_call(kernel, inputs, out_shape, scratch_shapes, limit, scalars=1, cost=None, space=pltpu.VMEM):
    specs = [pl.BlockSpec(memory_space=pltpu.SMEM)] * scalars
    specs += [pl.BlockSpec(memory_space=space)] * (len(inputs) - scalars)
    return pl.pallas_call(
        kernel,
        out_shape=out_shape,
        in_specs=specs,
        out_specs=jax.tree.map(lambda _: pl.BlockSpec(memory_space=pltpu.VMEM), out_shape),
        scratch_shapes=scratch_shapes,
        compiler_params=pltpu.CompilerParams(vmem_limit_bytes=limit),
        cost_estimate=cost,
    )(*inputs)


def place(x, y, z, core):
    return ((z % 4 * 8 + y * 2 + core) * 8) + x * 2 + z // 4


def turn_route(dx, way):
    return [
        (place(x, y, z, core), place((x + dx) % 4, y, (z + 2 - 4 * ((core + way) % 2)) % 8, core))
        for x, y, z, core in itertools.product(range(4), range(4), range(8), range(2))
    ]


def twin(matrix):
    zero = jnp.zeros_like(matrix)
    return jnp.concatenate(
        [jnp.concatenate([matrix, zero], axis=1), jnp.concatenate([zero, matrix], axis=1)], axis=0
    )


def shards(node_cells, node_frac, node_force, node_count, z_rates, z_synth, z_analysis):
    capacity = node_force.shape[0]
    slabs = lax.axis_size("gx")
    cos_base, sin_base = base_tables()
    full = np.block([[cos_base, sin_base], [-sin_base, cos_base]])
    y_table = split_table(full)[0]
    flip = np.eye(BASE)[::-1].astype(BF16)
    order = np.arange(BASE) ^ (BASE // 2)
    x_table = split_table(np.concatenate([cos_base, sin_base], axis=0)[:, order])[0]

    right, z_part, x_part, rim = vmem_call(
        prepare_kernel,
        (node_count, node_cells, node_frac, node_force.reshape(1, capacity)),
        (
            jax.ShapeDtypeStruct((ROWS, capacity), BF16),
            jax.ShapeDtypeStruct((NZ, capacity), F32),
            jax.ShapeDtypeStruct((56, capacity), F32),
            jax.ShapeDtypeStruct((ROWS, RADIX * NZ), BF16),
        ),
        [
            pltpu.VMEM((3, capacity), jnp.int32),
            pltpu.VMEM((3, capacity), F32),
            pltpu.VMEM((1, capacity), F32),
            pltpu.VMEM((RADIX * NZ, NODE_BLOCK), BF16),
            pltpu.VMEM((ROWS, RADIX * NZ), F32),
            pltpu.SemaphoreType.DMA((3,)),
        ],
        PREPARE_BYTES,
        space=pltpu.HBM,
        cost=pl.CostEstimate(flops=10**9, bytes_accessed=10**7, transcendentals=10**6),
    )
    rim = lax.ppermute(rim, "gx", [(i, (i + 1) % slabs) for i in range(slabs)])

    row = np.arange(BASE)
    angle = 2.0 * np.pi * np.outer(np.arange(1, 4), row) / NY
    y_cos = np.broadcast_to(np.cos(angle)[:, :, None], (3, BASE, LANES)).astype(np.float32)
    y_sin = np.broadcast_to(np.sin(angle)[:, :, None], (3, BASE, LANES)).astype(np.float32)

    tiles = vmem_call(
        spread_kernel,
        (node_count, right, z_part, x_part),
        jax.ShapeDtypeStruct((8, ROWS, WIDTH), BF16),
        [
            pltpu.VMEM((2 * WIDTH, SPREAD_BLOCK), BF16),
            pltpu.VMEM((8 * WIDTH, ROWS), F32),
        ],
        SPREAD_BYTES,
        cost=pl.CostEstimate(flops=10**10, bytes_accessed=10**7, transcendentals=0),
    )
    line = jax.ShapeDtypeStruct((ROWS, WIDTH), BF16)
    parts = vmem_call(sort_kernel, (tiles, rim), (line,) * 8, [], scalars=0, limit=SORT_BYTES)
    lines = [
        lax.ppermute(part, BOTH, turn_route(dx, way)) for part, (dx, way) in zip(parts, TURNS)
    ]
    spectrum = vmem_call(
        y_kernel,
        (*lines, y_table, flip, y_cos, y_sin),
        jax.ShapeDtypeStruct((BASE * ITEMS, LANES), BF16),
        [
            pltpu.VMEM((NY, WIDTH), F32),
            pltpu.VMEM((2 * BASE, 4 * WIDTH), BF16),
            pltpu.VMEM((BASE * ITEMS, LANES), F32),
        ],
        Y_BYTES,
        scalars=0,
        cost=pl.CostEstimate(flops=5 * 10**9, bytes_accessed=10**7, transcendentals=0),
    )
    packed = spectrum.reshape(BASE, ITEMS // 4, 4, LANES)
    moved = lax.all_to_all(packed, BOTH, split_axis=0, concat_axis=0, tiled=True)
    arrived = moved.transpose(1, 2, 0, 3).reshape(ITEMS, BASE, LANES)

    offset = np.arange(RADIX).reshape(3, 2)
    angle = 2.0 * np.pi * offset[:, None, :] * row[None, :, None] / NX
    x_cos = np.repeat(np.cos(angle), NZ, axis=2).astype(np.float32)
    x_sin = np.repeat(np.sin(angle), NZ, axis=2).astype(np.float32)
    number = row[None, :, None] + BASE * (np.arange(3)[:, None, None] + 3 * np.arange(2))
    across = np.repeat(4.0 * np.sin(np.pi * number / NX) ** 2, NZ, axis=2).astype(np.float32)
    first = (lax.axis_index("gx") * lax.axis_size("gy") + lax.axis_index("gy")) * RADIX
    y_number = (first + jnp.arange(RADIX, dtype=jnp.int32)).astype(F32)
    y_wave = jnp.sin(jnp.pi * y_number / NY)
    wave = 4.0 * y_wave * y_wave
    rates = jnp.concatenate([z_rates, z_rates]).reshape(1, LANES)

    def whole(array):
        return pl.BlockSpec(array.shape, lambda q: (0,) * array.ndim)

    constants = (
        x_table,
        x_cos,
        x_sin,
        across,
        rates,
        twin(z_analysis.T),
        twin(z_synth),
    )
    out = pl.pallas_call(
        x_kernel,
        out_shape=jax.ShapeDtypeStruct((2, RADIX, NZ, NX), F32),
        grid=(RADIX,),
        in_specs=[pl.BlockSpec((6, BASE, LANES), lambda q: (q, 0, 0))]
        + [pl.BlockSpec(memory_space=pltpu.SMEM)]
        + [whole(array) for array in constants],
        out_specs=pl.BlockSpec((2, 1, NZ, NX), lambda q: (0, q, 0, 0)),
        scratch_shapes=[
            pltpu.VMEM((2 * BASE, RADIX * LANES), F32),
            pltpu.VMEM((RADIX * BASE, 2 * LANES), BF16),
            pltpu.VMEM((RADIX * BASE, 2 * LANES), BF16),
            pltpu.VMEM((2 * LANES, 2 * LANES), BF16),
            pltpu.VMEM((2 * LANES, 2 * LANES), BF16),
        ],
        compiler_params=pltpu.CompilerParams(vmem_limit_bytes=X_BYTES),
    )(arrived, wave, *constants)
    return out.transpose(0, 2, 1, 3)


def solution(mesh):
    return jax.shard_map(
        shards,
        mesh=mesh,
        in_specs=(
            P(None, BOTH),
            P(None, BOTH),
            P(BOTH),
            P(BOTH),
            P(),
            P(),
            P(),
        ),
        out_specs=P(None, None, BOTH, None),
        check_vma=False,
    )
```

```python
import itertools
import math

import jax
import jax.numpy as jnp
import numpy as np
from jax import lax
from jax.experimental import pallas as pl
from jax.experimental.pallas import tpu as pltpu
from jax.sharding import PartitionSpec as P

NX = 1536
NY = 1536
WIN = 6
NZ = 64
RADIX = 6
BASE = 256
SLAB = 48
STRIP = 192
ROWS = 208
LANES = 128
UNROLL_X = 16
UNROLL_Y = 4
NODE_BLOCK = 1024
SPREAD_BLOCK = 2048
ITEMS = 36
WIDTH = 384
BOTH = ("gx", "gy")
TURNS = tuple((dx, way) for dx in (2, 1, 3, 0) for way in range(2))
F32 = jnp.float32
BF16 = jnp.bfloat16
HALF_ROOT3 = math.sqrt(3.0) / 2.0
MIB = 1024 * 1024
PREPARE_BYTES = 14 * MIB
SPREAD_BYTES = 20 * MIB
SORT_BYTES = 8 * MIB
Y_BYTES = 26 * MIB
X_BYTES = 26 * MIB


def split_table(table):
    high = table.astype(np.float32).astype(BF16)
    low = (table - high.astype(np.float64)).astype(np.float32).astype(BF16)
    return high, low


def base_tables():
    index = np.arange(BASE)
    angle = 2.0 * np.pi * (np.outer(index, index) % BASE) / BASE
    return np.cos(angle), np.sin(angle)


def split_value(value):
    high = value.astype(BF16)
    return high, (value - high.astype(F32)).astype(BF16)


def window(position, cell, frac):
    centred = (position - cell).astype(F32) - (WIN - 1) / 2.0
    distance = centred - frac
    inside = jnp.abs(centred) < WIN / 2.0
    return jnp.where(inside, jnp.exp(-0.5 * (distance * distance)), 0.0)


def dot_rows(left, right):
    return lax.dot_general(left, right, (((1,), (1,)), ((), ())), preferred_element_type=F32)


def matmul(left, right):
    return jnp.dot(left, right, preferred_element_type=F32)


def block_count(count_ref):
    return (count_ref[0] + (SPREAD_BLOCK - 1)) >> (SPREAD_BLOCK.bit_length() - 1)


def prepare_kernel(
    count_ref,
    cell_in,
    frac_in,
    force_in,
    right_ref,
    z_ref,
    x_ref,
    rim_ref,
    cell_ref,
    frac_ref,
    force_ref,
    left_ref,
    sum_ref,
    arrival,
):
    copies = [
        pltpu.make_async_copy(source, target, arrival.at[at])
        for at, (source, target) in enumerate(
            ((cell_in, cell_ref), (frac_in, frac_ref), (force_in, force_ref))
        )
    ]
    for copy in copies:
        copy.start()
    live_count = count_ref[0]
    capacity = force_ref.shape[1]
    scale = 8.0 / math.sqrt(capacity * 256)
    sum_ref[...] = jnp.zeros_like(sum_ref)
    for copy in copies:
        copy.wait()

    def body(block, carry):
        start = pl.multiple_of(block * NODE_BLOCK, NODE_BLOCK)
        span = pl.ds(start, NODE_BLOCK)

        def rows(extent):
            return lax.broadcasted_iota(jnp.int32, (extent, NODE_BLOCK), 0)

        slot = start + lax.broadcasted_iota(jnp.int32, (1, NODE_BLOCK), 1)
        amplitude = jnp.where(slot < live_count, force_ref[:, span] * scale, 0.0)
        z_part = amplitude * window(rows(NZ), cell_ref[2:3, span], frac_ref[2:3, span])
        x_part = window(rows(56), cell_ref[0:1, span], frac_ref[0:1, span])
        right = window(rows(ROWS), cell_ref[1:2, span], frac_ref[1:2, span]).astype(BF16)
        z_ref[:, span] = z_part
        x_ref[:, span] = x_part
        right_ref[:, span] = right
        for t in range(RADIX):
            left_ref[t * NZ : (t + 1) * NZ, :] = (
                z_part * x_part[SLAB + t : SLAB + t + 1, :]
            ).astype(BF16)
        sum_ref[...] += dot_rows(right, left_ref[...])
        return carry

    lax.fori_loop(0, block_count(count_ref) * (SPREAD_BLOCK // NODE_BLOCK), body, 0)
    rim_ref[...] = sum_ref[...].astype(BF16)


def spread_kernel(count_ref, right_ref, z_ref, x_ref, out_ref, left_ref, sum_ref):
    sum_ref[...] = jnp.zeros_like(sum_ref)

    def body(block, carry):
        span = pl.ds(pl.multiple_of(block * SPREAD_BLOCK, SPREAD_BLOCK), SPREAD_BLOCK)
        for pair in range(4):
            for k in range(2 * RADIX):
                x_at = pair * 2 * RADIX + k
                left_ref[k * NZ : (k + 1) * NZ, :] = (
                    z_ref[:, span] * x_ref[x_at : x_at + 1, span]
                ).astype(BF16)
            rows = slice(2 * pair * WIDTH, 2 * (pair + 1) * WIDTH)
            sum_ref[rows, :] += dot_rows(left_ref[...], right_ref[:, span])
        return carry

    lax.fori_loop(0, block_count(count_ref), body, 0)
    for j in range(8):
        out_ref[j] = sum_ref[j * WIDTH : (j + 1) * WIDTH, :].T.astype(BF16)


def partner(turn, sign):
    dx, way = TURNS[turn]
    gx, gy = lax.axis_index("gx"), lax.axis_index("gy")
    dz = 2 - 4 * ((gx + way) & 1)
    x_at = ((gy >> 1) + sign * dx) & 3
    z_at = ((gy & 1) * 4 + (gx >> 3) + sign * dz) & 7
    return x_at * 2 + (z_at >> 2)


def sort_kernel(in_ref, rim_ref, *out_refs):
    for turn, out_ref in enumerate(out_refs):
        block = partner(turn, 1)
        rim = jnp.where(block == 0, rim_ref[...].astype(F32), 0.0)
        out_ref[...] = (in_ref[block].astype(F32) + rim).astype(BF16)


def y_kernel(*refs):
    in_refs = refs[:8]
    table_ref, flip_ref, cos_ref, sin_ref, out_ref, grid_ref, th_ref, mode_ref = refs[8:]
    for turn in range(8):
        start = pl.multiple_of(partner(turn, -1) * STRIP, STRIP)
        grid_ref[pl.ds(start, STRIP), :] = in_refs[turn][0:STRIP, :].astype(F32)
    for turn in range(8):
        start = pl.multiple_of(((partner(turn, -1) + 1) & 7) * STRIP, STRIP)
        grid_ref[pl.ds(start, 16), :] += in_refs[turn][STRIP:ROWS, :].astype(F32)

    def body(step, carry):
        start = pl.multiple_of(step * 16, 16)
        for p in range(3):
            lanes = slice(p * LANES, (p + 1) * LANES)
            a = [grid_ref[pl.ds(n * BASE + start, 16), lanes] for n in range(RADIX)]
            s0, s1, s2 = a[0] + a[3], a[1] + a[4], a[2] + a[5]
            d0, d1, d2 = a[0] - a[3], a[1] - a[4], a[2] - a[5]
            turned = (
                (s0 + s1 + s2, None),
                (d0 + 0.5 * (d1 - d2), -HALF_ROOT3 * (d1 + d2)),
                (s0 - 0.5 * (s1 + s2), -HALF_ROOT3 * (s1 - s2)),
                (d0 - d1 + d2, None),
            )
            for q, (real, imag) in enumerate(turned):
                if q > 0:
                    cos = cos_ref[q - 1, pl.ds(start, 16), :]
                    sin = sin_ref[q - 1, pl.ds(start, 16), :]
                    if imag is None:
                        real, imag = real * cos, -real * sin
                    else:
                        real, imag = real * cos + imag * sin, imag * cos - real * sin
                else:
                    imag = jnp.zeros_like(real)
                columns = slice(q * WIDTH + p * LANES, q * WIDTH + (p + 1) * LANES)
                for at, value in ((0, real), (BASE, imag)):
                    th_ref[pl.ds(at + start, 16), columns] = value.astype(BF16)
        return carry

    lax.fori_loop(0, BASE // 16, body, 0, unroll=UNROLL_Y)

    def put(q, part, modes, first):
        for p in range(3):
            item = (q * 2 + part) * 3 + p
            lanes = slice(first + p * LANES, first + (p + 1) * LANES)
            mode_ref[pl.ds(item, BASE, stride=ITEMS), :] = modes[:, lanes]

    for first in (1, 0, 2, 3):
        columns = slice(first * WIDTH, (first + 1) * WIDTH)
        high = th_ref[:, columns]
        modes = matmul(table_ref[...], high)
        for part in range(2):
            rows = modes[part * BASE : (part + 1) * BASE]
            put(first, part, rows, 0)
            if first in (1, 2):
                mirror = matmul(flip_ref[...], rows.astype(BF16))
                put(RADIX - first, part, mirror if part == 0 else -mirror, 0)
    out_ref[...] = mode_ref[...].astype(BF16)


def x_kernel(
    in_ref,
    wave_ref,
    table_ref,
    cos_ref,
    sin_ref,
    across_ref,
    rate_ref,
    analysis_ref,
    synth_ref,
    out_ref,
    modes_ref,
    x_ref,
    c_ref,
    wa_ref,
    ws_ref,
):
    q = pl.program_id(0)

    @pl.when(q == 0)
    def _():
        high, low = split_value(analysis_ref[...])
        for k in range(2):
            wa_ref[k * LANES : (k + 1) * LANES, :LANES] = high
            wa_ref[k * LANES : (k + 1) * LANES, LANES:] = low
        high, low = split_value(synth_ref[...])
        for k in range(2):
            ws_ref[:LANES, k * LANES : (k + 1) * LANES] = high
            ws_ref[LANES:, k * LANES : (k + 1) * LANES] = low

    lane = lax.broadcasted_iota(jnp.int32, (16, LANES), 1)
    lower = lane < NZ
    sign = jnp.where(lower, 1.0, -1.0)
    turn_1r = jnp.where(lower, 1.0, 0.5)
    turn_2r = jnp.where(lower, 1.0, -0.5)
    turn_i = jnp.where(lower, 0.0, -HALF_ROOT3)

    def one_wave(k):
        lines = jnp.concatenate([in_ref[6 * k + item] for item in range(6)], axis=1)
        modes_ref[k] = matmul(table_ref[...], lines)

        def body(step, carry):
            start = pl.multiple_of(step * 16, 16)
            real, imag = [], []
            for xp in range(3):
                at_real = slice(xp * LANES, (xp + 1) * LANES)
                at_imag = slice((3 + xp) * LANES, (4 + xp) * LANES)
                mode_real = (
                    modes_ref[k, pl.ds(start, 16), at_real] + modes_ref[k, pl.ds(BASE + start, 16), at_imag]
                )
                mode_imag = (
                    modes_ref[k, pl.ds(start, 16), at_imag] - modes_ref[k, pl.ds(BASE + start, 16), at_real]
                )
                cos = cos_ref[xp, pl.ds(start, 16), :]
                sin = sin_ref[xp, pl.ds(start, 16), :]
                real.append(mode_real * cos + mode_imag * sin)
                imag.append(mode_imag * cos - mode_real * sin)
            sum_r, sum_i = real[1] + real[2], imag[1] + imag[2]
            dif_r, dif_i = HALF_ROOT3 * (real[1] - real[2]), HALF_ROOT3 * (imag[1] - imag[2])
            mid_r, mid_i = real[0] - 0.5 * sum_r, imag[0] - 0.5 * sum_i
            u1r, u1i = mid_r + dif_i, mid_i - dif_r
            u2r, u2i = mid_r - dif_i, mid_i + dif_r
            thirds = (
                (real[0] + sum_r, imag[0] + sum_i),
                (u1r * turn_1r - u1i * turn_i, u1i * turn_1r + u1r * turn_i),
                (u2r * turn_2r - u2i * turn_i, u2i * turn_2r + u2r * turn_i),
            )
            for m in range(3):
                for part in range(2):
                    value = thirds[m][part]
                    value = pltpu.roll(value, NZ, 1) + sign * value
                    high, low = split_value(value)
                    row = pl.ds((m * 2 + part) * BASE + start, 16)
                    x_ref[k, row, :LANES] = high
                    x_ref[k, row, LANES:] = low
            return carry

        lax.fori_loop(0, BASE // 16, body, 0, unroll=UNROLL_X)
        shift = rate_ref[...] + wave_ref[2 * q + k]
        both = matmul(x_ref[k], wa_ref[...])
        for m in range(3):
            inverse = 1.0 / (across_ref[m] + shift)
            for part in range(2):
                rows = slice((m * 2 + part) * BASE, (m * 2 + part + 1) * BASE)
                high, low = split_value((both[rows, :LANES] + both[rows, LANES:]) * inverse)
                c_ref[k, rows, :LANES] = high
                c_ref[k, rows, LANES:] = low
        both = dot_rows(ws_ref[...], c_ref[k])
        value = both[:LANES] + both[LANES:]
        for m in range(3):
            for part in range(2):
                columns = slice((m * 2 + part) * BASE, (m * 2 + part + 1) * BASE)
                out_ref[part, k, :, m * BASE : (m + 1) * BASE] = value[:NZ, columns]
                out_ref[part, k, :, (m + 3) * BASE : (m + 4) * BASE] = value[NZ:, columns]

    for k in range(2):
        one_wave(k)


def vmem_call(kernel, inputs, out_shape, scratch_shapes, limit, scalars=1, cost=None, space=pltpu.VMEM):
    specs = [pl.BlockSpec(memory_space=pltpu.SMEM)] * scalars
    specs += [pl.BlockSpec(memory_space=space)] * (len(inputs) - scalars)
    return pl.pallas_call(
        kernel,
        out_shape=out_shape,
        in_specs=specs,
        out_specs=jax.tree.map(lambda _: pl.BlockSpec(memory_space=pltpu.VMEM), out_shape),
        scratch_shapes=scratch_shapes,
        compiler_params=pltpu.CompilerParams(vmem_limit_bytes=limit),
        cost_estimate=cost,
    )(*inputs)


def place(x, y, z, core):
    return ((z % 4 * 8 + y * 2 + core) * 8) + x * 2 + z // 4


def turn_route(dx, way):
    return [
        (place(x, y, z, core), place((x + dx) % 4, y, (z + 2 - 4 * ((core + way) % 2)) % 8, core))
        for x, y, z, core in itertools.product(range(4), range(4), range(8), range(2))
    ]


def twin(matrix):
    zero = jnp.zeros_like(matrix)
    return jnp.concatenate(
        [jnp.concatenate([matrix, zero], axis=1), jnp.concatenate([zero, matrix], axis=1)], axis=0
    )


def shards(node_cells, node_frac, node_force, node_count, z_rates, z_synth, z_analysis):
    capacity = node_force.shape[0]
    slabs = lax.axis_size("gx")
    cos_base, sin_base = base_tables()
    full = np.block([[cos_base, sin_base], [-sin_base, cos_base]])
    y_table = split_table(full)[0]
    flip = np.eye(BASE)[::-1].astype(BF16)
    order = np.arange(BASE) ^ (BASE // 2)
    x_table = split_table(np.concatenate([cos_base, sin_base], axis=0)[:, order])[0]

    right, z_part, x_part, rim = vmem_call(
        prepare_kernel,
        (node_count, node_cells, node_frac, node_force.reshape(1, capacity)),
        (
            jax.ShapeDtypeStruct((ROWS, capacity), BF16),
            jax.ShapeDtypeStruct((NZ, capacity), F32),
            jax.ShapeDtypeStruct((56, capacity), F32),
            jax.ShapeDtypeStruct((ROWS, RADIX * NZ), BF16),
        ),
        [
            pltpu.VMEM((3, capacity), jnp.int32),
            pltpu.VMEM((3, capacity), F32),
            pltpu.VMEM((1, capacity), F32),
            pltpu.VMEM((RADIX * NZ, NODE_BLOCK), BF16),
            pltpu.VMEM((ROWS, RADIX * NZ), F32),
            pltpu.SemaphoreType.DMA((3,)),
        ],
        PREPARE_BYTES,
        space=pltpu.HBM,
        cost=pl.CostEstimate(flops=10**9, bytes_accessed=10**7, transcendentals=10**6),
    )
    rim = lax.ppermute(rim, "gx", [(i, (i + 1) % slabs) for i in range(slabs)])

    row = np.arange(BASE)
    angle = 2.0 * np.pi * np.outer(np.arange(1, 4), row) / NY
    y_cos = np.broadcast_to(np.cos(angle)[:, :, None], (3, BASE, LANES)).astype(np.float32)
    y_sin = np.broadcast_to(np.sin(angle)[:, :, None], (3, BASE, LANES)).astype(np.float32)

    tiles = vmem_call(
        spread_kernel,
        (node_count, right, z_part, x_part),
        jax.ShapeDtypeStruct((8, ROWS, WIDTH), BF16),
        [
            pltpu.VMEM((2 * WIDTH, SPREAD_BLOCK), BF16),
            pltpu.VMEM((8 * WIDTH, ROWS), F32),
        ],
        SPREAD_BYTES,
        cost=pl.CostEstimate(flops=10**10, bytes_accessed=10**7, transcendentals=0),
    )
    line = jax.ShapeDtypeStruct((ROWS, WIDTH), BF16)
    parts = vmem_call(sort_kernel, (tiles, rim), (line,) * 8, [], scalars=0, limit=SORT_BYTES)
    lines = [
        lax.ppermute(part, BOTH, turn_route(dx, way)) for part, (dx, way) in zip(parts, TURNS)
    ]
    spectrum = vmem_call(
        y_kernel,
        (*lines, y_table, flip, y_cos, y_sin),
        jax.ShapeDtypeStruct((BASE * ITEMS, LANES), BF16),
        [
            pltpu.VMEM((NY, WIDTH), F32),
            pltpu.VMEM((2 * BASE, 4 * WIDTH), BF16),
            pltpu.VMEM((BASE * ITEMS, LANES), F32),
        ],
        Y_BYTES,
        scalars=0,
        cost=pl.CostEstimate(flops=5 * 10**9, bytes_accessed=10**7, transcendentals=0),
    )
    packed = spectrum.reshape(BASE, ITEMS // 4, 4, LANES)
    moved = lax.all_to_all(packed, BOTH, split_axis=0, concat_axis=0, tiled=True)
    arrived = moved.transpose(1, 2, 0, 3).reshape(ITEMS, BASE, LANES)

    offset = np.arange(RADIX).reshape(3, 2)
    angle = 2.0 * np.pi * offset[:, None, :] * row[None, :, None] / NX
    x_cos = np.repeat(np.cos(angle), NZ, axis=2).astype(np.float32)
    x_sin = np.repeat(np.sin(angle), NZ, axis=2).astype(np.float32)
    number = row[None, :, None] + BASE * (np.arange(3)[:, None, None] + 3 * np.arange(2))
    across = np.repeat(4.0 * np.sin(np.pi * number / NX) ** 2, NZ, axis=2).astype(np.float32)
    first = (lax.axis_index("gx") * lax.axis_size("gy") + lax.axis_index("gy")) * RADIX
    y_number = (first + jnp.arange(RADIX, dtype=jnp.int32)).astype(F32)
    y_wave = jnp.sin(jnp.pi * y_number / NY)
    wave = 4.0 * y_wave * y_wave
    rates = jnp.concatenate([z_rates, z_rates]).reshape(1, LANES)

    def whole(array):
        return pl.BlockSpec(array.shape, lambda q: (0,) * array.ndim)

    constants = (
        x_table,
        x_cos,
        x_sin,
        across,
        rates,
        twin(z_analysis.T),
        twin(z_synth),
    )
    out = pl.pallas_call(
        x_kernel,
        out_shape=jax.ShapeDtypeStruct((2, RADIX, NZ, NX), F32),
        grid=(RADIX // 2,),
        in_specs=[pl.BlockSpec((12, BASE, LANES), lambda q: (q, 0, 0))]
        + [pl.BlockSpec(memory_space=pltpu.SMEM)]
        + [whole(array) for array in constants],
        out_specs=pl.BlockSpec((2, 2, NZ, NX), lambda q: (0, q, 0, 0)),
        scratch_shapes=[
            pltpu.VMEM((2, 2 * BASE, RADIX * LANES), F32),
            pltpu.VMEM((2, RADIX * BASE, 2 * LANES), BF16),
            pltpu.VMEM((2, RADIX * BASE, 2 * LANES), BF16),
            pltpu.VMEM((2 * LANES, 2 * LANES), BF16),
            pltpu.VMEM((2 * LANES, 2 * LANES), BF16),
        ],
        compiler_params=pltpu.CompilerParams(vmem_limit_bytes=X_BYTES),
    )(arrived, wave, *constants)
    return out.transpose(0, 2, 1, 3)


def solution(mesh):
    return jax.shard_map(
        shards,
        mesh=mesh,
        in_specs=(
            P(None, BOTH),
            P(None, BOTH),
            P(BOTH),
            P(BOTH),
            P(),
            P(),
            P(),
        ),
        out_specs=P(None, None, BOTH, None),
        check_vma=False,
    )
```
